1024 devices in a mesh: dom: 64 (over x, z), feat: 16 (over y, core).
Axes of the slice: x: 8, y: 8, z: 8, core: 2. Of those that a mesh axis runs over, the one named last changes fastest.
Arguments:
- node_feats: bfloat16 [16384, 1024], P('dom', 'feat'), may hold values from -6 to 6
- history: bfloat16 [16384, 1024], P('dom', 'feat'), may hold values from -6 to 6
- halo_blocks: int32 [64, 32], replicated, may hold values from 0 to 127, as said below
- tile_index: int32 [128, 24], P('dom'), may hold values from 0 to 33, as said below
- tile_weight: bfloat16 [128, 24, 128, 128], P('dom'), may hold values from 0.001 to 10, as said below
- self_one: bfloat16 [1024, 1024], P(None, 'feat'), may hold values from -0.1875 to 0.1875
- neigh_one: bfloat16 [1024, 1024], P(None, 'feat'), may hold values from -3 to 3
- self_two: bfloat16 [1024, 1024], P(None, 'feat'), may hold values from -0.1875 to 0.1875
- neigh_two: bfloat16 [1024, 1024], P(None, 'feat'), may hold values from -3 to 3
- batch_ids: int32 [8192], P('dom'), may hold values from 0 to 255
- cotangent: bfloat16 [8192, 1024], P('dom', 'feat'), may hold values from -0.06591797 to 0.06591797
Outputs:
- node_out: bfloat16 [16384, 1024], P('dom', 'feat')
- grad_self_one: float32 [1024, 1024], P(None, 'feat')
- grad_neigh_one: float32 [1024, 1024], P(None, 'feat')
- grad_self_two: float32 [1024, 1024], P(None, 'feat')
- grad_neigh_two: float32 [1024, 1024], P(None, 'feat')
The draws below stay inside these ranges and needn't reach their ends.
Inputs may be any that keep to these rules, and one draw needn't show every extreme that they name: `halo_blocks`: row p names 32 blocks that belong to 32 different partitions, none of them p: exactly one block from each partition it reads; some partitions are read by far more partitions than others. `tile_index`: each partition's tiles together name every one of its 34 table blocks. `tile_weight`: positive edge weights.
All inputs are finite; a program needn't handle non-finite values.
Results may differ from the reference program's by a relative error of at most 0.024.
Values may be sent and summed in bfloat16 or wider, within the bound.
No kernel may reach another device: no remote copies, remote signals or barrier semaphores. Data moves between devices by JAX's collectives and lax.ppermute only.
A program may use at most 32 MiB of HBM per device.

```python
import math
import jax
import jax.numpy as jnp
from jax import lax

H = 1024
BLOCK = 128
K = 24
B_DEV = 2
BATCH_DEV = 128
HALO = 32
ROWS_DEV = 256
NODES = 16384
BATCH = 8192
N_DOM = 64
N_FEAT = 16


def draw_halo_blocks(key, part):
    key = jax.random.fold_in(key, 11)
    key_heat, key_noise, key_local = jax.random.split(key, 3)
    popularity = jax.random.randint(key_heat, (N_DOM,), 0, 4)
    random_jitter = jax.random.randint(key_noise, (N_DOM, N_DOM), 0, 1 << 20)
    owner_parts = jnp.arange(N_DOM, dtype=jnp.int32)[None, :]
    readers = jnp.arange(N_DOM, dtype=jnp.int32)[:, None]
    leading_couple = (readers == 0) & (owner_parts == N_DOM - 1)
    trailing_couple = (readers == N_DOM - 1) & (owner_parts == 0)
    extra_reward = jnp.where(leading_couple | trailing_couple, 8, 0)
    ranking_values = (random_jitter + (popularity[None, :] + extra_reward) * (1 << 20)) * N_DOM + owner_parts
    ranking_values = jnp.where(owner_parts == readers, -1, ranking_values)
    unused_values, chosen = lax.top_k(ranking_values, HALO)
    chosen = chosen.astype(jnp.int32)
    local_block = jax.random.randint(key_local, (N_DOM, HALO), 0, B_DEV)
    row_ids = jnp.arange(N_DOM, dtype=jnp.int32)[:, None]
    local_block = jnp.where((row_ids == 0) & (chosen == N_DOM - 1), B_DEV - 1, local_block)
    local_block = jnp.where((row_ids == N_DOM - 1) & (chosen == 0), 0, local_block)
    return (chosen * B_DEV + local_block).astype(jnp.int32)


def draw_tile_index(key, part):
    key = jax.random.fold_in(key, 23)
    part_keys = jax.random.split(key, N_DOM)

    def per_part(part_key):
        key_cover, key_extra, key_order = jax.random.split(part_key, 3)
        cover = jax.random.permutation(key_cover, B_DEV + HALO).astype(jnp.int32)
        extra = jax.random.randint(key_extra, (B_DEV * K - B_DEV - HALO,), 0, B_DEV + HALO).astype(jnp.int32)
        joined = jnp.concatenate([cover, extra])
        return jax.random.permutation(key_order, joined).reshape(B_DEV, K)
    return jax.vmap(per_part)(part_keys).reshape(N_DOM * B_DEV, K).astype(jnp.int32)


def draw_tile_weight(key, part):
    key = jax.random.fold_in(key, 37)
    key_rows, key_base = jax.random.split(key)
    shape = (N_DOM * B_DEV, K, BLOCK, BLOCK)
    row_scale = jnp.exp(jax.random.uniform(key_rows, (N_DOM * B_DEV, 1, BLOCK, 1), jnp.float32, 0.0, math.log(10.0)))
    base = jnp.exp(jax.random.uniform(key_base, shape, jnp.float32, math.log(0.001), 0.0))
    return jnp.clip(base * row_scale, 0.001, 10.0).astype(jnp.bfloat16)


def place_ends(array, rng, least, high):
    shape = array.shape
    spot = [jax.random.randint(jax.random.fold_in(rng, axis), (), 0, shape[axis]) for axis in range(len(shape))]
    array = array.at[tuple(spot)].set(least)
    longest = shape.index(max(shape))
    spot[longest] = (spot[longest] + 1) % shape[longest]
    return array.at[tuple(spot)].set(high)


def shard_levels(key, dims, cuts, low, top_value):
    level = 1.0
    for dim, shards_of in cuts:
        heights = jax.random.uniform(jax.random.fold_in(jax.random.fold_in(key, 6), dim), (shards_of,), jnp.float32, low / len(cuts), top_value / len(cuts))
        level = level * jnp.repeat(jnp.exp(heights), dims[dim] // shards_of).reshape((-1,) + (1,) * (len(dims) - 1 - dim))
    return level


def normal_values(rng, extent, spread, bound, shards=(), kind=jnp.bfloat16):
    loudness = shard_levels(rng, extent, shards, -0.22, 0.18) if shards else 1.0
    entries = jax.random.normal(rng, extent, jnp.float32) * spread * loudness
    return jnp.minimum(jnp.maximum(entries, -bound), bound).astype(kind)


def setup_inputs(seed: int = 0) -> dict:
    streams_of = jax.random.split(jax.random.key(seed), 12)
    return {
        "node_feats": normal_values(streams_of[0], (NODES, H), 1.0, 6.0, ((0, 64), (1, 16))),
        "history": normal_values(streams_of[1], (NODES, H), 1.0, 6.0, ((0, 64), (1, 16))),
        "halo_blocks": draw_halo_blocks(jax.random.fold_in(streams_of[11], 71), 0),
        "tile_index": draw_tile_index(jax.random.fold_in(streams_of[11], 71), 0),
        "tile_weight": draw_tile_weight(jax.random.fold_in(streams_of[11], 71), 0),
        "self_one": normal_values(streams_of[5], (H, H), H ** -0.5, 0.1875, ((1, 16),)),
        "neigh_one": normal_values(streams_of[6], (H, H), (16 * H ** -0.5), 3.0, ((1, 16),)),
        "self_two": normal_values(streams_of[7], (H, H), H ** -0.5, 0.1875, ((1, 16),)),
        "neigh_two": normal_values(streams_of[8], (H, H), (16 * H ** -0.5), 3.0, ((1, 16),)),
        "batch_ids": place_ends(jax.random.randint(streams_of[9], (BATCH,), 0, ROWS_DEV), jax.random.fold_in(streams_of[9], 1), 0, ROWS_DEV - 1).astype(jnp.int32),
        "cotangent": normal_values(streams_of[10], (BATCH, H), (BATCH ** -0.5), 0.06591797, ((0, 64), (1, 16))),
    }


def aggregate(source_rows, tile_index, tile_weight):
    picked = source_rows[tile_index]
    weights = tile_weight.astype(jnp.float32)
    summed = jnp.einsum('bkvc,bkcf->bvf', weights, picked.astype(jnp.float32))
    row_total = lax.optimization_barrier(jnp.sum(weights, axis=(1, 3)))
    return ((summed / row_total[:, :, None]).astype(jnp.bfloat16), row_total)

def neighbour_means(own_rows, remote_rows, halo_blocks, tile_index, tile_weight):

    def per_part(values):
        own_part, wanted, index_part, weight_part = values
        source_rows = jnp.concatenate([own_part, remote_rows[wanted]], axis=0)
        return aggregate(source_rows, index_part, weight_part)
    return lax.map(per_part, (own_rows, halo_blocks, tile_index, tile_weight))

def spread_back(scaled, tile_index, tile_weight):

    def per_part(values):
        index_part, weight_part, scaled_part = values
        contrib = jnp.einsum('bkvc,bvf->bkcf', weight_part.astype(jnp.float32), scaled_part.astype(jnp.float32))
        onehot = (index_part[:, :, None] == jnp.arange(B_DEV, dtype=jnp.int32)[None, None, :]).astype(jnp.float32)
        return jnp.einsum('bkn,bkcf->ncf', onehot, contrib, precision=lax.Precision.HIGHEST)
    return lax.map(per_part, (tile_index, tile_weight, scaled))

def reference(node_feats, history, halo_blocks, tile_index, tile_weight, self_one, neigh_one, self_two, neigh_two, batch_ids, cotangent):
    all_blocks = N_DOM * B_DEV
    index_parts = tile_index.reshape(N_DOM, B_DEV, K)
    weight_parts = tile_weight.reshape(N_DOM, B_DEV, K, BLOCK, BLOCK)
    agg_one, row_total = neighbour_means(node_feats.reshape(N_DOM, B_DEV, BLOCK, H), node_feats.reshape(all_blocks, BLOCK, H), halo_blocks, index_parts, weight_parts)
    agg_one = agg_one.reshape(NODES, H)
    pre_one = jnp.dot(node_feats, self_one, preferred_element_type=jnp.float32) + jnp.dot(agg_one, neigh_one, preferred_element_type=jnp.float32)
    hidden_one = jax.nn.silu(pre_one).astype(jnp.bfloat16)
    agg_two, unused_total = neighbour_means(hidden_one.reshape(N_DOM, B_DEV, BLOCK, H), history.reshape(all_blocks, BLOCK, H), halo_blocks, index_parts, weight_parts)
    agg_two = agg_two.reshape(NODES, H)
    pre_two = jnp.dot(hidden_one, self_two, preferred_element_type=jnp.float32) + jnp.dot(agg_two, neigh_two, preferred_element_type=jnp.float32)
    node_out = pre_two.astype(jnp.bfloat16)
    targets = jnp.arange(BATCH, dtype=jnp.int32) // BATCH_DEV * ROWS_DEV + batch_ids.astype(jnp.int32)
    grad_two = jnp.zeros((NODES, H), jnp.float32).at[targets].add(cotangent.astype(jnp.float32)).astype(jnp.bfloat16)
    grad_self_two = jnp.dot(hidden_one.T, grad_two, preferred_element_type=jnp.float32)
    grad_neigh_two = jnp.dot(agg_two.T, grad_two, preferred_element_type=jnp.float32)
    slice_width = H // N_FEAT
    back_self = jnp.zeros((NODES, H), jnp.float32)
    back_neigh = jnp.zeros((NODES, H), jnp.float32)
    for piece_id in range(N_FEAT):
        lower = piece_id * slice_width
        grad_piece = grad_two[:, lower:lower + slice_width]
        term_self = jnp.dot(grad_piece, self_two[:, lower:lower + slice_width].T, preferred_element_type=jnp.float32).astype(jnp.bfloat16)
        term_neigh = jnp.dot(grad_piece, neigh_two[:, lower:lower + slice_width].T, preferred_element_type=jnp.float32).astype(jnp.bfloat16)
        back_self = back_self + lax.optimization_barrier(term_self).astype(jnp.float32)
        back_neigh = back_neigh + lax.optimization_barrier(term_neigh).astype(jnp.float32)
    scaled = (back_neigh.reshape(N_DOM, B_DEV, BLOCK, H) / row_total[:, :, :, None]).astype(jnp.bfloat16)
    own_grad = spread_back(scaled, index_parts, weight_parts).reshape(NODES, H)
    unused_out, pull = jax.vjp(jax.nn.silu, pre_one)
    grad_one = pull(back_self + own_grad)[0].astype(jnp.bfloat16)
    grad_self_one = jnp.dot(node_feats.T, grad_one, preferred_element_type=jnp.float32)
    grad_neigh_one = jnp.dot(agg_one.T, grad_one, preferred_element_type=jnp.float32)
    return (node_out, grad_self_one, grad_neigh_one, grad_self_two, grad_neigh_two)
```

```python
import jax
import jax.numpy as jnp
from jax import lax
from jax.sharding import PartitionSpec as P

BF = jnp.bfloat16
F32 = jnp.float32


def mm(a, b, dims):
    return lax.dot_general(a, b, (dims, ((), ())), preferred_element_type=F32)


def on_device(
    node_feats,
    history,
    halo_blocks,
    tile_index,
    tile_weight,
    self_one,
    neigh_one,
    self_two,
    neigh_two,
    batch_ids,
    cotangent,
):
    own_blocks, tiles = tile_index.shape
    rows = tile_weight.shape[2]
    width = node_feats.shape[1]
    owned = node_feats.shape[0]
    parts = halo_blocks.shape[0]
    seeds = cotangent.shape[0]
    me = lax.axis_index("dom")

    feats_t = node_feats.T
    cot_t = cotangent.T
    self_one_t, neigh_one_t, self_two_t, neigh_two_t = (
        self_one.T,
        neigh_one.T,
        self_two.T,
        neigh_two.T,
    )

    def blocks_first(array_t):
        return array_t.reshape(width, own_blocks, rows).transpose(1, 0, 2)

    all_history = lax.all_gather(blocks_first(history.T), "dom", axis=0, tiled=True)
    whole = lax.all_gather(jnp.concatenate([feats_t, cot_t], axis=1), "feat", axis=0, tiled=True)
    whole_feats, whole_cot = whole[:, :owned], whole[:, owned:]

    feat_blocks = blocks_first(feats_t)
    second = jnp.any(halo_blocks == own_blocks * me + 1, axis=1)
    send = jnp.where(second[:, None, None], feat_blocks[1][None], feat_blocks[0][None])
    got = lax.all_to_all(send, "dom", 0, 0, tiled=True)

    wanted = lax.dynamic_index_in_dim(halo_blocks, me, 0, keepdims=False)
    is_own = tile_index < own_blocks
    tile_block = wanted[jnp.clip(tile_index - own_blocks, 0, wanted.shape[0] - 1)]
    tile_block = jnp.clip(tile_block, 0, own_blocks * parts - 1)

    onehot = tile_index[:, :, None] == jnp.arange(own_blocks, dtype=jnp.int32)[None, None, :]
    dense = jnp.sum(
        jnp.where(onehot[:, :, :, None, None], tile_weight[:, :, None].astype(F32), 0.0), axis=1
    )
    dense = dense.transpose(0, 2, 1, 3).reshape(owned, owned).astype(BF)
    row_total = jnp.sum(tile_weight, axis=(1, 3), dtype=F32).reshape(1, owned)
    inverse = 1.0 / row_total

    def halo_sum(picked):
        picked = jnp.where(is_own[:, :, None, None], jnp.zeros((), BF), picked)
        out = jnp.einsum("bkfc,bkvc->fbv", picked, tile_weight, preferred_element_type=F32)
        return out.reshape(width, owned)

    both = jnp.concatenate(
        [
            self_two_t.reshape(width, -1, width).transpose(1, 0, 2),
            neigh_two_t.reshape(width, -1, width).transpose(1, 0, 2),
        ],
        axis=2,
    )
    columns = lax.all_to_all(both, "feat", 0, 0, tiled=True).reshape(-1, 2 * width)

    mean_one = (halo_sum(got[tile_block // own_blocks]) + mm(feats_t, dense, ((1,), (1,)))) * inverse
    whole_mean_one = lax.all_gather(mean_one.astype(BF), "feat", axis=0, tiled=True)
    pre_one = mm(self_one_t, whole_feats, ((1,), (0,))) + mm(
        neigh_one_t, whole_mean_one, ((1,), (0,))
    )
    gate = jax.nn.sigmoid(pre_one)
    hidden = (pre_one * gate).astype(BF)

    whole_hidden = lax.all_gather(hidden, "feat", axis=0, tiled=True)
    halo_two = (halo_sum(all_history[tile_block]) * inverse).astype(BF)
    whole_halo_two = lax.all_gather(halo_two, "feat", axis=0, tiled=True)
    whole_mean_two = (
        mm(whole_hidden, dense, ((1,), (1,))) * inverse + whole_halo_two.astype(F32)
    ).astype(BF)
    node_out = mm(self_two_t, whole_hidden, ((1,), (0,))) + mm(
        neigh_two_t, whole_mean_two, ((1,), (0,))
    )

    seed_rows = (
        batch_ids[:, None] == jnp.arange(owned, dtype=jnp.int32)[None, :]
    ).astype(BF)
    whole_grad_two = mm(whole_cot, seed_rows, ((1,), (0,))).astype(BF)
    grad_two = mm(cot_t, seed_rows, ((1,), (0,))).astype(BF)
    back = mm(columns, whole_grad_two, ((0,), (0,)))
    scaled = (back[width:] * inverse).astype(BF)
    own_grad = mm(scaled, dense, ((1,), (0,)))
    slope = gate * (1.0 + pre_one * (1.0 - gate))
    grad_one = ((back[:width] + own_grad) * slope).astype(BF)
    ones = mm(
        grad_one, jnp.concatenate([whole_feats, whole_mean_one], axis=0), ((1,), (1,))
    )
    twos = mm(
        grad_two, jnp.concatenate([whole_hidden, whole_mean_two], axis=0), ((1,), (1,))
    )
    total = jnp.concatenate([ones, twos], axis=1).astype(BF)
    depth = self_one.shape[0]
    low, high = 8, width // 8
    wide = parts // high
    lanes = depth // wide
    pieces = total.reshape(high, low, 4, wide, lanes).transpose(0, 3, 2, 1, 4)
    pieces = pieces.reshape(parts, 4, low, lanes)
    mine = lax.all_to_all(pieces, "dom", 0, 0, tiled=True)
    mine = jnp.sum(mine.astype(F32), axis=0, keepdims=True).astype(BF)
    spread = jnp.broadcast_to(mine, (parts, 4, low, lanes))
    sums = lax.all_to_all(spread, "dom", 0, 0, tiled=True)
    sums = sums.reshape(high, wide, 4, low, lanes).transpose(2, 0, 3, 1, 4)
    sums = sums.reshape(4, width, depth).astype(F32)
    return (
        node_out.astype(BF).T,
        sums[0].T,
        sums[1].T,
        sums[2].T,
        sums[3].T,
    )


def solution(mesh):
    return jax.shard_map(
        on_device,
        mesh=mesh,
        in_specs=(
            P("dom", "feat"),
            P("dom", "feat"),
            P(),
            P("dom", None),
            P("dom", None, None, None),
            P(None, "feat"),
            P(None, "feat"),
            P(None, "feat"),
            P(None, "feat"),
            P("dom"),
            P("dom", "feat"),
        ),
        out_specs=(
            P("dom", "feat"),
            P(None, "feat"),
            P(None, "feat"),
            P(None, "feat"),
            P(None, "feat"),
        ),
        check_vma=False,
    )
```

```python
import jax
import jax.numpy as jnp
from jax import lax
from jax.experimental.layout import Layout, with_layout_constraint
from jax.sharding import PartitionSpec as P

BF = jnp.bfloat16
F32 = jnp.float32


def mm(a, b, dims):
    return lax.dot_general(a, b, (dims, ((), ())), preferred_element_type=F32)


def after(value, *others):
    return lax.optimization_barrier((value, *others))[0]


def on_device(
    node_feats,
    history,
    halo_blocks,
    tile_index,
    tile_weight,
    self_one,
    neigh_one,
    self_two,
    neigh_two,
    batch_ids,
    cotangent,
):
    own_blocks, tiles = tile_index.shape
    rows = tile_weight.shape[2]
    width = node_feats.shape[1]
    owned = node_feats.shape[0]
    parts = halo_blocks.shape[0]
    seeds = cotangent.shape[0]
    me = lax.axis_index("dom")

    feats_t = node_feats.T
    cot_t = cotangent.T
    self_one_t, neigh_one_t, self_two_t, neigh_two_t = (
        self_one.T,
        neigh_one.T,
        self_two.T,
        neigh_two.T,
    )

    second = jnp.any(halo_blocks == own_blocks * me + 1, axis=1)[:, None, None]

    def pick(array_t):
        return jnp.where(second, array_t[None, :, rows:], array_t[None, :, :rows])

    send_feats, self_two_t, neigh_two_t = lax.optimization_barrier(
        (pick(feats_t), self_two_t, neigh_two_t)
    )
    halo_feats = lax.all_to_all(send_feats, "dom", 0, 0, tiled=True)
    whole = lax.all_gather(jnp.concatenate([feats_t, cot_t], axis=1), "feat", axis=0, tiled=True)
    whole_feats, whole_cot = whole[:, :owned], whole[:, owned:]

    wanted = lax.dynamic_index_in_dim(halo_blocks, me, 0, keepdims=False)
    is_own = tile_index < own_blocks
    tile_block = wanted[jnp.clip(tile_index - own_blocks, 0, wanted.shape[0] - 1)]
    tile_owner = jnp.clip(tile_block // own_blocks, 0, parts - 1)

    onehot = tile_index[:, :, None] == jnp.arange(own_blocks, dtype=jnp.int32)[None, None, :]
    dense = jnp.sum(
        jnp.where(onehot[:, :, :, None, None], tile_weight[:, :, None].astype(F32), 0.0), axis=1
    )
    dense = dense.transpose(0, 2, 1, 3).reshape(owned, owned).astype(BF)
    row_total = jnp.sum(tile_weight, axis=(1, 3), dtype=F32).reshape(1, owned)
    inverse = 1.0 / row_total

    def halo_sum(picked):
        picked = jnp.where(is_own[:, :, None, None], jnp.zeros((), BF), picked)
        out = jnp.einsum("bkfc,bkvc->fbv", picked, tile_weight, preferred_element_type=F32)
        return out.reshape(width, owned)

    both = jnp.concatenate(
        [
            self_two_t.reshape(width, -1, width).transpose(1, 0, 2),
            neigh_two_t.reshape(width, -1, width).transpose(1, 0, 2),
        ],
        axis=2,
    )
    both = with_layout_constraint(both, Layout(major_to_minor=(0, 1, 2)))
    columns = lax.all_gather(both, "feat", axis=0, tiled=False)
    columns = lax.dynamic_index_in_dim(columns, lax.axis_index("feat"), 1, keepdims=False)
    columns = columns.reshape(-1, 2 * width)

    send_history = after(pick(history.T), whole, dense, inverse, halo_feats)
    halo_history = lax.all_to_all(send_history, "dom", 0, 0, tiled=True)

    mean_one = (halo_sum(halo_feats[tile_owner]) + mm(feats_t, dense, ((1,), (1,)))) * inverse
    whole_mean_one = lax.all_gather(mean_one.astype(BF), "feat", axis=0, tiled=True)
    pre_one = mm(self_one_t, whole_feats, ((1,), (0,))) + mm(
        neigh_one_t, whole_mean_one, ((1,), (0,))
    )
    gate = jax.nn.sigmoid(pre_one)
    hidden = (pre_one * gate).astype(BF)

    whole_hidden = lax.all_gather(hidden, "feat", axis=0, tiled=True)
    seed_rows = (
        batch_ids[:, None] == jnp.arange(owned, dtype=jnp.int32)[None, :]
    ).astype(BF)
    whole_grad_two = mm(whole_cot, seed_rows, ((1,), (0,))).astype(BF)
    grad_two = mm(cot_t, seed_rows, ((1,), (0,))).astype(BF)
    back = mm(columns, whole_grad_two, ((0,), (0,)))
    scaled = (back[width:] * inverse).astype(BF)
    own_grad = mm(scaled, dense, ((1,), (0,)))
    slope = gate * (1.0 + pre_one * (1.0 - gate))
    grad_one = ((back[:width] + own_grad) * slope).astype(BF)
    depth = self_one.shape[0]
    low, high = 8, width // 8
    wide = parts // high
    lanes = depth // wide

    def pieces_of(total):
        n = total.shape[1] // depth
        pieces = total.astype(BF).reshape(high, low, n, wide, lanes).transpose(0, 3, 2, 1, 4)
        return pieces.reshape(parts, n, low, lanes)

    def summed(pieces):
        got = lax.all_to_all(pieces, "dom", 0, 0, tiled=True)
        return jnp.sum(got.astype(F32), axis=0, keepdims=True).astype(BF)

    ones = mm(
        grad_one, jnp.concatenate([whole_feats, whole_mean_one], axis=0), ((1,), (1,))
    )
    self_part = mm(grad_two, whole_hidden, ((1,), (1,)))
    first = pieces_of(jnp.concatenate([ones, self_part], axis=1))
    halo_history = after(halo_history, whole_hidden, first)
    first = after(first, halo_history)
    halo_two = (halo_sum(halo_history[tile_owner]) * inverse).astype(BF)
    whole_halo_two = lax.all_gather(halo_two, "feat", axis=0, tiled=True)
    whole_mean_two = (
        mm(whole_hidden, dense, ((1,), (1,))) * inverse + whole_halo_two.astype(F32)
    ).astype(BF)
    node_out = mm(self_two_t, whole_hidden, ((1,), (0,))) + mm(
        neigh_two_t, whole_mean_two, ((1,), (0,))
    )

    last = pieces_of(mm(grad_two, whole_mean_two, ((1,), (1,))))
    first = summed(first)
    mine = jnp.concatenate([first, summed(after(last, first))], axis=1)
    spread = jnp.broadcast_to(mine, (parts, *mine.shape[1:]))
    sums = lax.all_to_all(spread, "dom", 0, 0, tiled=True)
    sums = sums.reshape(high, wide, -1, low, lanes).transpose(2, 0, 3, 1, 4)
    sums = sums.reshape(-1, width, depth).astype(F32)
    return (node_out.astype(BF).T, sums[0].T, sums[1].T, sums[2].T, sums[3].T)


def solution(mesh):
    return jax.shard_map(
        on_device,
        mesh=mesh,
        in_specs=(
            P("dom", "feat"),
            P("dom", "feat"),
            P(),
            P("dom", None),
            P("dom", None, None, None),
            P(None, "feat"),
            P(None, "feat"),
            P(None, "feat"),
            P(None, "feat"),
            P("dom"),
            P("dom", "feat"),
        ),
        out_specs=(
            P("dom", "feat"),
            P(None, "feat"),
            P(None, "feat"),
            P(None, "feat"),
            P(None, "feat"),
        ),
        check_vma=False,
    )
```

```python
import jax
import jax.numpy as jnp
from jax import lax
from jax.experimental.layout import Layout, with_layout_constraint
from jax.sharding import PartitionSpec as P

BF = jnp.bfloat16
F32 = jnp.float32


def mm(a, b, dims):
    return lax.dot_general(a, b, (dims, ((), ())), preferred_element_type=F32)


def after(value, *others):
    return lax.optimization_barrier((value, *others))[0]


def on_device(
    node_feats,
    history,
    halo_blocks,
    tile_index,
    tile_weight,
    self_one,
    neigh_one,
    self_two,
    neigh_two,
    batch_ids,
    cotangent,
):
    own_blocks, tiles = tile_index.shape
    rows = tile_weight.shape[2]
    width = node_feats.shape[1]
    owned = node_feats.shape[0]
    parts = halo_blocks.shape[0]
    seeds = cotangent.shape[0]
    me = lax.axis_index("dom")

    feats_t = node_feats.T
    cot_t = cotangent.T
    self_one_t, neigh_one_t, self_two_t, neigh_two_t = (
        self_one.T,
        neigh_one.T,
        self_two.T,
        neigh_two.T,
    )

    second = jnp.any(halo_blocks == own_blocks * me + 1, axis=1)[:, None, None]

    def pick(array_t):
        return jnp.where(second, array_t[None, :, rows:], array_t[None, :, :rows])

    send_feats, feats_t, self_two_t, neigh_two_t = lax.optimization_barrier(
        (pick(feats_t), feats_t, self_two_t, neigh_two_t)
    )
    halo_feats = lax.all_to_all(send_feats, "dom", 0, 0, tiled=True)
    wanted = lax.dynamic_index_in_dim(halo_blocks, me, 0, keepdims=False)
    is_own = tile_index < own_blocks
    tile_block = wanted[jnp.clip(tile_index - own_blocks, 0, wanted.shape[0] - 1)]
    tile_owner = jnp.clip(tile_block // own_blocks, 0, parts - 1)

    onehot = tile_index[:, :, None] == jnp.arange(own_blocks, dtype=jnp.int32)[None, None, :]
    dense = jnp.sum(
        jnp.where(onehot[:, :, :, None, None], tile_weight[:, :, None].astype(F32), 0.0), axis=1
    )
    dense = dense.transpose(0, 2, 1, 3).reshape(owned, owned).astype(BF)
    row_total = jnp.sum(tile_weight, axis=(1, 3), dtype=F32).reshape(1, owned)
    inverse = 1.0 / row_total

    def halo_sum(picked):
        picked = jnp.where(is_own[:, :, None, None], jnp.zeros((), BF), picked)
        out = jnp.einsum("bkfc,bkvc->fbv", picked, tile_weight, preferred_element_type=F32)
        return out.reshape(width, owned)

    side = jnp.concatenate(
        [
            feats_t.reshape(width, own_blocks, rows).transpose(1, 0, 2),
            cot_t.reshape(width, 1, seeds).transpose(1, 0, 2),
            jnp.concatenate(
                [
                    self_two_t.reshape(width, -1, width).transpose(1, 0, 2),
                    neigh_two_t.reshape(width, -1, width).transpose(1, 0, 2),
                ],
                axis=2,
            ),
        ],
        axis=0,
    )
    side = with_layout_constraint(side, Layout(major_to_minor=(0, 1, 2)))
    whole = lax.all_gather(side, "feat", axis=0, tiled=False)
    whole_feats = jnp.concatenate(
        [whole[:, i].reshape(-1, rows) for i in range(own_blocks)], axis=1
    )
    whole_cot = whole[:, own_blocks].reshape(-1, seeds)
    columns = lax.dynamic_index_in_dim(
        whole, own_blocks + 1 + lax.axis_index("feat"), 1, keepdims=False
    ).reshape(-1, 2 * width)

    send_history = after(pick(history.T), dense, inverse, halo_feats)
    halo_history = lax.all_to_all(send_history, "dom", 0, 0, tiled=True)

    mean_one = (halo_sum(halo_feats[tile_owner]) + mm(feats_t, dense, ((1,), (1,)))) * inverse
    whole_mean_one = lax.all_gather(mean_one.astype(BF), "feat", axis=0, tiled=True)
    pre_one = mm(self_one_t, whole_feats, ((1,), (0,))) + mm(
        neigh_one_t, whole_mean_one, ((1,), (0,))
    )
    gate = jax.nn.sigmoid(pre_one)
    hidden = (pre_one * gate).astype(BF)

    whole_hidden = lax.all_gather(hidden, "feat", axis=0, tiled=True)
    seed_rows = (
        batch_ids[:, None] == jnp.arange(owned, dtype=jnp.int32)[None, :]
    ).astype(BF)
    whole_grad_two = mm(whole_cot, seed_rows, ((1,), (0,))).astype(BF)
    grad_two = mm(cot_t, seed_rows, ((1,), (0,))).astype(BF)
    back = mm(columns, whole_grad_two, ((0,), (0,)))
    scaled = (back[width:] * inverse).astype(BF)
    own_grad = mm(scaled, dense, ((1,), (0,)))
    slope = gate * (1.0 + pre_one * (1.0 - gate))
    grad_one = ((back[:width] + own_grad) * slope).astype(BF)
    depth = self_one.shape[0]
    low, high = 8, width // 8
    wide = parts // high
    lanes = depth // wide

    def pieces_of(total):
        n = total.shape[1] // depth
        pieces = total.astype(BF).reshape(high, low, n, wide, lanes).transpose(0, 3, 2, 1, 4)
        return pieces.reshape(parts, n, low, lanes)

    halo_history = after(halo_history, whole_hidden)
    halo_two = (halo_sum(halo_history[tile_owner]) * inverse).astype(BF)
    whole_halo_two = lax.all_gather(halo_two, "feat", axis=0, tiled=True)
    whole_mean_two = (
        mm(whole_hidden, dense, ((1,), (1,))) * inverse + whole_halo_two.astype(F32)
    ).astype(BF)
    node_out = mm(self_two_t, whole_hidden, ((1,), (0,))) + mm(
        neigh_two_t, whole_mean_two, ((1,), (0,))
    )

    ones = mm(
        grad_one, jnp.concatenate([whole_feats, whole_mean_one], axis=0), ((1,), (1,))
    )
    twos = mm(
        grad_two, jnp.concatenate([whole_hidden, whole_mean_two], axis=0), ((1,), (1,))
    )
    mine = lax.all_to_all(
        pieces_of(jnp.concatenate([ones, twos], axis=1)), "dom", 0, 0, tiled=True
    )
    mine = jnp.sum(mine.astype(F32), axis=0, keepdims=True).astype(BF)
    spread = jnp.broadcast_to(mine, (parts, *mine.shape[1:]))
    sums = lax.all_to_all(spread, "dom", 0, 0, tiled=True)
    sums = sums.reshape(high, wide, -1, low, lanes).transpose(2, 0, 3, 1, 4)
    sums = sums.reshape(-1, width, depth).astype(F32)
    return (node_out.astype(BF).T, sums[0].T, sums[1].T, sums[2].T, sums[3].T)


def solution(mesh):
    return jax.shard_map(
        on_device,
        mesh=mesh,
        in_specs=(
            P("dom", "feat"),
            P("dom", "feat"),
            P(),
            P("dom", None),
            P("dom", None, None, None),
            P(None, "feat"),
            P(None, "feat"),
            P(None, "feat"),
            P(None, "feat"),
            P("dom"),
            P("dom", "feat"),
        ),
        out_specs=(
            P("dom", "feat"),
            P(None, "feat"),
            P(None, "feat"),
            P(None, "feat"),
            P(None, "feat"),
        ),
        check_vma=False,
    )
```

```python
import jax
import jax.numpy as jnp
from jax import lax
from jax.experimental import pallas as pl
from jax.experimental.layout import Layout, with_layout_constraint
from jax.sharding import PartitionSpec as P

BF = jnp.bfloat16
F32 = jnp.float32


def mm(a, b, dims):
    return lax.dot_general(a, b, (dims, ((), ())), preferred_element_type=F32)


def after(value, *others):
    return lax.optimization_barrier((value, *others))[0]


def add_and_copy(got_ref, out_ref):
    total = jnp.sum(got_ref[...].astype(F32), axis=0, keepdims=True)
    out_ref[...] = jnp.broadcast_to(total.astype(out_ref.dtype), out_ref.shape)


def unpack(sums_ref, self_one_ref, neigh_one_ref, self_two_ref, neigh_two_ref):
    parts, _, low, lanes = sums_ref.shape
    width, depth = self_one_ref.shape
    high = width // low
    wide = depth // lanes
    for i in range(high):
        down = slice(i * low, (i + 1) * low)
        for j in range(wide):
            across = slice(j * lanes, (j + 1) * lanes)
            base = i * 2 * wide + j
            self_one_ref[down, across] = sums_ref[base, 0].astype(F32)
            neigh_one_ref[down, across] = sums_ref[base + wide, 0].astype(F32)
            left = sums_ref[2 * j * high + i, 1].astype(F32)
            right = sums_ref[(2 * j + 1) * high + i, 1].astype(F32)
            self_two_ref[down, across] = jnp.concatenate(
                [left[:, :width], right[:, :width]], axis=1
            )
            neigh_two_ref[down, across] = jnp.concatenate(
                [left[:, width:], right[:, width:]], axis=1
            )


def on_device(
    node_feats,
    history,
    halo_blocks,
    tile_index,
    tile_weight,
    self_one,
    neigh_one,
    self_two,
    neigh_two,
    batch_ids,
    cotangent,
):
    own_blocks, tiles = tile_index.shape
    rows = tile_weight.shape[2]
    width = node_feats.shape[1]
    owned = node_feats.shape[0]
    parts = halo_blocks.shape[0]
    seeds = cotangent.shape[0]
    me = lax.axis_index("dom")

    feats_t = node_feats.T
    cot_t = cotangent.T
    self_one_t, neigh_one_t, self_two_t, neigh_two_t = (
        self_one.T,
        neigh_one.T,
        self_two.T,
        neigh_two.T,
    )

    second = jnp.any(halo_blocks == own_blocks * me + 1, axis=1)[:, None, None]

    def pick(array_t):
        return jnp.where(second, array_t[None, :, rows:], array_t[None, :, :rows])

    send_feats, feats_t, self_two_t, neigh_two_t = lax.optimization_barrier(
        (pick(feats_t), feats_t, self_two_t, neigh_two_t)
    )
    halo_feats = lax.all_to_all(send_feats, "dom", 0, 0, tiled=True)
    wanted = lax.dynamic_index_in_dim(halo_blocks, me, 0, keepdims=False)
    is_own = tile_index < own_blocks
    tile_block = wanted[jnp.clip(tile_index - own_blocks, 0, wanted.shape[0] - 1)]
    tile_owner = jnp.clip(tile_block // own_blocks, 0, parts - 1)

    onehot = tile_index[:, :, None] == jnp.arange(own_blocks, dtype=jnp.int32)[None, None, :]
    dense = jnp.sum(
        jnp.where(onehot[:, :, :, None, None], tile_weight[:, :, None].astype(F32), 0.0), axis=1
    )
    dense = dense.transpose(0, 2, 1, 3).reshape(owned, owned).astype(BF)
    row_total = jnp.sum(tile_weight, axis=(1, 3), dtype=F32).reshape(1, owned)
    inverse = 1.0 / row_total

    def halo_sum(picked):
        picked = jnp.where(is_own[:, :, None, None], jnp.zeros((), BF), picked)
        out = jnp.einsum("bkfc,bkvc->fbv", picked, tile_weight, preferred_element_type=F32)
        return out.reshape(width, owned)

    side = jnp.concatenate(
        [
            feats_t.reshape(width, own_blocks, rows).transpose(1, 0, 2),
            cot_t.reshape(width, 1, seeds).transpose(1, 0, 2),
            jnp.concatenate(
                [
                    self_two_t.reshape(width, -1, width).transpose(1, 0, 2),
                    neigh_two_t.reshape(width, -1, width).transpose(1, 0, 2),
                ],
                axis=2,
            ),
        ],
        axis=0,
    )
    side = with_layout_constraint(side, Layout(major_to_minor=(0, 1, 2)))
    whole = lax.all_gather(side, "feat", axis=0, tiled=False)
    whole_feats = jnp.concatenate(
        [whole[:, i].reshape(-1, rows) for i in range(own_blocks)], axis=1
    )
    whole_cot = whole[:, own_blocks].reshape(-1, seeds)
    columns = lax.dynamic_index_in_dim(
        whole, own_blocks + 1 + lax.axis_index("feat"), 1, keepdims=False
    ).reshape(-1, 2 * width)

    send_history = after(pick(history.T), dense, inverse, halo_feats)
    halo_history = lax.all_to_all(send_history, "dom", 0, 0, tiled=True)

    mean_one = (halo_sum(halo_feats[tile_owner]) + mm(feats_t, dense, ((1,), (1,)))) * inverse
    whole_mean_one = lax.all_gather(mean_one.astype(BF), "feat", axis=0, tiled=True)
    pre_one = mm(self_one_t, whole_feats, ((1,), (0,))) + mm(
        neigh_one_t, whole_mean_one, ((1,), (0,))
    )
    gate = jax.nn.sigmoid(pre_one)
    hidden = (pre_one * gate).astype(BF)

    seed_rows = (
        batch_ids[:, None] == jnp.arange(owned, dtype=jnp.int32)[None, :]
    ).astype(BF)
    whole_grad_two = mm(whole_cot, seed_rows, ((1,), (0,))).astype(BF)
    back = mm(columns, whole_grad_two, ((0,), (0,)))
    scaled = (back[width:] * inverse).astype(BF)
    own_grad = mm(scaled, dense, ((1,), (0,)))
    slope = gate * (1.0 + pre_one * (1.0 - gate))
    grad_one = ((back[:width] + own_grad) * slope).astype(BF)
    ones = mm(
        grad_one, jnp.concatenate([whole_feats, whole_mean_one], axis=0), ((1,), (1,))
    )
    depth = self_one.shape[0]
    lanes = 2 * width
    high = parts * lanes // (2 * depth)
    low = width // high
    ones = ones.astype(BF).reshape(high, low, 2 * depth // lanes, lanes).transpose(0, 2, 1, 3)
    ones = ones.reshape(parts, 1, low, lanes)

    halo_history = after(halo_history, ones)
    mean_two = (
        (halo_sum(halo_history[tile_owner]) + mm(hidden, dense, ((1,), (1,)))) * inverse
    ).astype(BF)
    layer_two = jnp.concatenate([hidden, mean_two], axis=0)

    twos = mm(whole_grad_two, layer_two, ((1,), (1,))).astype(BF)
    slices = depth // width
    twos = lax.all_to_all(twos.reshape(slices, width, 2 * width), "feat", 0, 0, tiled=True)
    whole_two = lax.all_gather(after(layer_two, twos), "feat", axis=0, tiled=False)
    pieces = jnp.concatenate([ones, twos.reshape(parts, 1, low, lanes)], axis=1)
    got = lax.all_to_all(pieces, "dom", 0, 0, tiled=True)
    spread = pl.pallas_call(add_and_copy, out_shape=jax.ShapeDtypeStruct(got.shape, BF))(got)
    sums = lax.all_to_all(spread, "dom", 0, 0, tiled=True)
    grads = pl.pallas_call(
        unpack, out_shape=[jax.ShapeDtypeStruct((width, depth), F32)] * 4
    )(sums)

    whole_hidden = whole_two[:, :width].reshape(depth, owned)
    whole_mean_two = whole_two[:, width:].reshape(depth, owned)
    node_out = mm(self_two_t, whole_hidden, ((1,), (0,))) + mm(
        neigh_two_t, whole_mean_two, ((1,), (0,))
    )
    return (node_out.astype(BF).T, *[grad.T for grad in grads])


def solution(mesh):
    return jax.shard_map(
        on_device,
        mesh=mesh,
        in_specs=(
            P("dom", "feat"),
            P("dom", "feat"),
            P(),
            P("dom", None),
            P("dom", None, None, None),
            P(None, "feat"),
            P(None, "feat"),
            P(None, "feat"),
            P(None, "feat"),
            P("dom"),
            P("dom", "feat"),
        ),
        out_specs=(
            P("dom", "feat"),
            P(None, "feat"),
            P(None, "feat"),
            P(None, "feat"),
            P(None, "feat"),
        ),
        check_vma=False,
    )
```

```python
import jax
import jax.numpy as jnp
from jax import lax
from jax.experimental import pallas as pl
from jax.experimental.pallas import tpu as pltpu
from jax.experimental.layout import Layout, with_layout_constraint
from jax.sharding import PartitionSpec as P

BF = jnp.bfloat16
F32 = jnp.float32


def mm(a, b, dims):
    return lax.dot_general(a, b, (dims, ((), ())), preferred_element_type=F32)


def after(value, *others):
    return lax.optimization_barrier((value, *others))[0]


CHUNKS = 4


def pick_blocks(second_ref, halo_ref, rows_ref, out_ref, picked, sems):
    parts, _, lanes = picked.shape
    names = jnp.where(halo_ref[...] == second_ref[0], 1.0, 0.0)
    names = jnp.max(names, axis=0, keepdims=True)
    names = jnp.broadcast_to(names, (lanes, parts)).T
    low = rows_ref[:, :lanes].astype(F32)
    high = rows_ref[:, lanes:].astype(F32)
    step = parts // CHUNKS
    copies = []
    for chunk in range(CHUNKS):
        for reader in range(chunk * step, (chunk + 1) * step):
            name = jnp.broadcast_to(names[reader : reader + 1, :], low.shape)
            picked[reader] = jnp.where(name > 0.5, high, low).astype(picked.dtype)
        part = pl.ds(chunk * step, step)
        copy = pltpu.make_async_copy(picked.at[part], out_ref.at[part], sems.at[chunk])
        copy.start()
        copies.append(copy)
    for copy in copies:
        copy.wait()


def unpack(sums_any, self_one_ref, neigh_one_ref, self_two_ref, neigh_two_ref, sums_ref):
    pltpu.sync_copy(sums_any, sums_ref)
    parts, _, low, lanes = sums_ref.shape
    width, depth = self_one_ref.shape
    high = width // low
    wide = depth // lanes
    for i in range(high):
        down = slice(i * low, (i + 1) * low)
        for j in range(wide):
            across = slice(j * lanes, (j + 1) * lanes)
            base = i * 2 * wide + j
            self_one_ref[down, across] = sums_ref[base, 0].astype(F32)
            neigh_one_ref[down, across] = sums_ref[base + wide, 0].astype(F32)
            left = sums_ref[2 * j * high + i, 1].astype(F32)
            right = sums_ref[(2 * j + 1) * high + i, 1].astype(F32)
            self_two_ref[down, across] = jnp.concatenate(
                [left[:, :width], right[:, :width]], axis=1
            )
            neigh_two_ref[down, across] = jnp.concatenate(
                [left[:, width:], right[:, width:]], axis=1
            )


def on_device(
    node_feats,
    history,
    halo_blocks,
    tile_index,
    tile_weight,
    self_one,
    neigh_one,
    self_two,
    neigh_two,
    batch_ids,
    cotangent,
):
    own_blocks, tiles = tile_index.shape
    rows = tile_weight.shape[2]
    width = node_feats.shape[1]
    owned = node_feats.shape[0]
    parts = halo_blocks.shape[0]
    seeds = cotangent.shape[0]
    me = lax.axis_index("dom")

    feats_t = node_feats.T
    cot_t = cotangent.T
    self_one_t, neigh_one_t, self_two_t, neigh_two_t = (
        self_one.T,
        neigh_one.T,
        self_two.T,
        neigh_two.T,
    )

    second = own_blocks * me + 1
    send_feats = pl.pallas_call(
        pick_blocks,
        in_specs=[
            pl.BlockSpec(memory_space=pltpu.SMEM),
            pl.BlockSpec(memory_space=pltpu.VMEM),
            pl.BlockSpec(memory_space=pltpu.VMEM),
        ],
        out_specs=pl.BlockSpec(memory_space=pl.ANY),
        out_shape=jax.ShapeDtypeStruct((parts, width, rows), BF),
        scratch_shapes=[
            pltpu.VMEM((parts, width, rows), BF),
            pltpu.SemaphoreType.DMA((CHUNKS,)),
        ],
    )(second.reshape(1).astype(jnp.int32), halo_blocks.T, feats_t)
    send_feats, feats_t, self_two_t, neigh_two_t = lax.optimization_barrier(
        (send_feats, feats_t, self_two_t, neigh_two_t)
    )
    halo_feats = lax.all_to_all(send_feats, "dom", 0, 0, tiled=True)
    wanted = lax.dynamic_index_in_dim(halo_blocks, me, 0, keepdims=False)
    is_own = tile_index < own_blocks
    tile_block = wanted[jnp.clip(tile_index - own_blocks, 0, wanted.shape[0] - 1)]
    tile_owner = jnp.clip(tile_block // own_blocks, 0, parts - 1)

    onehot = tile_index[:, :, None] == jnp.arange(own_blocks, dtype=jnp.int32)[None, None, :]
    dense = jnp.sum(
        jnp.where(onehot[:, :, :, None, None], tile_weight[:, :, None].astype(F32), 0.0), axis=1
    )
    dense = dense.transpose(0, 2, 1, 3).reshape(owned, owned).astype(BF)
    row_total = jnp.sum(tile_weight, axis=(1, 3), dtype=F32).reshape(1, owned)
    inverse = 1.0 / row_total

    def halo_sum(picked):
        picked = jnp.where(is_own[:, :, None, None], jnp.zeros((), BF), picked)
        out = jnp.einsum("bkfc,bkvc->fbv", picked, tile_weight, preferred_element_type=F32)
        return out.reshape(width, owned)

    side = jnp.concatenate(
        [
            feats_t.reshape(width, own_blocks, rows).transpose(1, 0, 2),
            cot_t.reshape(width, 1, seeds).transpose(1, 0, 2),
            jnp.concatenate(
                [
                    self_two_t.reshape(width, -1, width).transpose(1, 0, 2),
                    neigh_two_t.reshape(width, -1, width).transpose(1, 0, 2),
                ],
                axis=2,
            ),
        ],
        axis=0,
    )
    side = with_layout_constraint(side, Layout(major_to_minor=(0, 1, 2)))
    whole = lax.all_gather(side, "feat", axis=0, tiled=False)
    whole_feats = jnp.concatenate(
        [whole[:, i].reshape(-1, rows) for i in range(own_blocks)], axis=1
    )
    whole_cot = whole[:, own_blocks].reshape(-1, seeds)
    columns = lax.dynamic_index_in_dim(
        whole, own_blocks + 1 + lax.axis_index("feat"), 1, keepdims=False
    ).reshape(-1, 2 * width)

    history_t, halo_late = after((history.T, halo_blocks), dense)
    named = jnp.any(halo_late == second, axis=1)[:, None, None]
    send_history = jnp.where(named, history_t[None, :, rows:], history_t[None, :, :rows])
    send_history = after(send_history, inverse, halo_feats)
    halo_history = lax.all_to_all(send_history, "dom", 0, 0, tiled=True)

    mean_one = (halo_sum(halo_feats[tile_owner]) + mm(feats_t, dense, ((1,), (1,)))) * inverse
    whole_mean_one = lax.all_gather(mean_one.astype(BF), "feat", axis=0, tiled=True)
    pre_one = mm(self_one_t, whole_feats, ((1,), (0,))) + mm(
        neigh_one_t, whole_mean_one, ((1,), (0,))
    )
    gate = jax.nn.sigmoid(pre_one)
    hidden = (pre_one * gate).astype(BF)

    seed_rows = (
        batch_ids[:, None] == jnp.arange(owned, dtype=jnp.int32)[None, :]
    ).astype(BF)
    whole_grad_two = mm(whole_cot, seed_rows, ((1,), (0,))).astype(BF)
    back = mm(columns, whole_grad_two, ((0,), (0,)))
    scaled = (back[width:] * inverse).astype(BF)
    own_grad = mm(scaled, dense, ((1,), (0,)))
    slope = gate * (1.0 + pre_one * (1.0 - gate))
    grad_one = ((back[:width] + own_grad) * slope).astype(BF)
    ones = mm(
        grad_one, jnp.concatenate([whole_feats, whole_mean_one], axis=0), ((1,), (1,))
    )
    depth = self_one.shape[0]
    lanes = 2 * width
    high = parts * lanes // (2 * depth)
    low = width // high
    ones = ones.astype(BF).reshape(high, low, 2 * depth // lanes, lanes).transpose(0, 2, 1, 3)
    ones = ones.reshape(parts, 1, low, lanes)

    halo_history = after(halo_history, ones)
    mean_two = (
        (halo_sum(halo_history[tile_owner]) + mm(hidden, dense, ((1,), (1,)))) * inverse
    ).astype(BF)
    layer_two = jnp.concatenate([hidden, mean_two], axis=0)

    twos = mm(whole_grad_two, layer_two, ((1,), (1,))).astype(BF)
    slices = depth // width
    twos = lax.all_to_all(twos.reshape(slices, width, 2 * width), "feat", 0, 0, tiled=True)
    whole_two = lax.all_gather(after(layer_two, twos), "feat", axis=0, tiled=False)
    pieces = jnp.concatenate([ones, twos.reshape(parts, 1, low, lanes)], axis=1)
    pieces = with_layout_constraint(pieces, Layout(major_to_minor=(0, 1, 2, 3)))
    got = lax.all_to_all(pieces, "dom", 0, 0, tiled=True)
    mine = jnp.sum(got.astype(F32), axis=0, keepdims=True).astype(BF)
    spread = jnp.broadcast_to(mine, pieces.shape)
    sums = lax.all_to_all(spread, "dom", 0, 0, tiled=True)
    grads = pl.pallas_call(
        unpack,
        in_specs=[pl.BlockSpec(memory_space=pl.ANY)],
        out_shape=[jax.ShapeDtypeStruct((width, depth), F32)] * 4,
        scratch_shapes=[pltpu.VMEM(sums.shape, BF)],
    )(sums)

    whole_hidden = whole_two[:, :width].reshape(depth, owned)
    whole_mean_two = whole_two[:, width:].reshape(depth, owned)
    node_out = mm(self_two_t, whole_hidden, ((1,), (0,))) + mm(
        neigh_two_t, whole_mean_two, ((1,), (0,))
    )
    return (node_out.astype(BF).T, *[grad.T for grad in grads])


def solution(mesh):
    return jax.shard_map(
        on_device,
        mesh=mesh,
        in_specs=(
            P("dom", "feat"),
            P("dom", "feat"),
            P(),
            P("dom", None),
            P("dom", None, None, None),
            P(None, "feat"),
            P(None, "feat"),
            P(None, "feat"),
            P(None, "feat"),
            P("dom"),
            P("dom", "feat"),
        ),
        out_specs=(
            P("dom", "feat"),
            P(None, "feat"),
            P(None, "feat"),
            P(None, "feat"),
            P(None, "feat"),
        ),
        check_vma=False,
    )
```

```python
import jax
import jax.numpy as jnp
from jax import lax
from jax.experimental import pallas as pl
from jax.experimental.pallas import tpu as pltpu
from jax.experimental.layout import Layout, with_layout_constraint
from jax.sharding import PartitionSpec as P

BF = jnp.bfloat16
F32 = jnp.float32


def mm(a, b, dims):
    return lax.dot_general(a, b, (dims, ((), ())), preferred_element_type=F32)


CHUNKS = 4


def lay_out(
    second_ref, halo_ref, rows_ref, seeds_ref, self_ref, neigh_ref, out_ref, side_ref, picked, sems
):
    parts, width, lanes = picked.shape
    names = jnp.where(halo_ref[...] == second_ref[0], 1.0, 0.0)
    names = jnp.max(names, axis=0, keepdims=True)
    names = jnp.broadcast_to(names, (lanes, parts)).T
    low = rows_ref[:, :lanes].astype(F32)
    high = rows_ref[:, lanes:].astype(F32)
    step = parts // CHUNKS
    copies = []
    for chunk in range(CHUNKS):
        for reader in range(chunk * step, (chunk + 1) * step):
            name = jnp.broadcast_to(names[reader : reader + 1, :], low.shape)
            picked[reader] = jnp.where(name > 0.5, high, low).astype(picked.dtype)
        part = pl.ds(chunk * step, step)
        copy = pltpu.make_async_copy(picked.at[part], out_ref.at[part], sems.at[chunk])
        copy.start()
        copies.append(copy)
    side_ref[0] = rows_ref[:, :lanes]
    side_ref[1] = rows_ref[:, lanes:]
    side_ref[2] = seeds_ref[...]
    for pair in range(self_ref.shape[1] // lanes):
        across = slice(pair * lanes, (pair + 1) * lanes)
        own = self_ref[:, across].astype(F32)
        near = neigh_ref[:, across].astype(F32)
        left = jnp.concatenate([own[:, :width], near[:, :width]], axis=1)
        right = jnp.concatenate([own[:, width:], near[:, width:]], axis=1)
        side_ref[3 + 2 * pair] = left.astype(side_ref.dtype)
        side_ref[4 + 2 * pair] = right.astype(side_ref.dtype)
    for copy in copies:
        copy.wait()


def unpack(sums_any, self_one_ref, neigh_one_ref, self_two_ref, neigh_two_ref, sums_ref):
    pltpu.sync_copy(sums_any, sums_ref)
    parts, _, low, lanes = sums_ref.shape
    width, depth = self_one_ref.shape
    high = width // low
    wide = depth // lanes
    for i in range(high):
        down = slice(i * low, (i + 1) * low)
        for j in range(wide):
            across = slice(j * lanes, (j + 1) * lanes)
            base = i * 2 * wide + j
            self_one_ref[down, across] = sums_ref[base, 0].astype(F32)
            neigh_one_ref[down, across] = sums_ref[base + wide, 0].astype(F32)
            left = sums_ref[2 * j * high + i, 1].astype(F32)
            right = sums_ref[(2 * j + 1) * high + i, 1].astype(F32)
            self_two_ref[down, across] = jnp.concatenate(
                [left[:, :width], right[:, :width]], axis=1
            )
            neigh_two_ref[down, across] = jnp.concatenate(
                [left[:, width:], right[:, width:]], axis=1
            )


def on_device(
    node_feats,
    history,
    halo_blocks,
    tile_index,
    tile_weight,
    self_one,
    neigh_one,
    self_two,
    neigh_two,
    batch_ids,
    cotangent,
):
    own_blocks, tiles = tile_index.shape
    rows = tile_weight.shape[2]
    width = node_feats.shape[1]
    owned = node_feats.shape[0]
    parts = halo_blocks.shape[0]
    seeds = cotangent.shape[0]
    me = lax.axis_index("dom")

    feats_t = node_feats.T
    cot_t = cotangent.T
    self_one_t, neigh_one_t, self_two_t, neigh_two_t = (
        self_one.T,
        neigh_one.T,
        self_two.T,
        neigh_two.T,
    )

    second = own_blocks * me + 1
    slices = self_two_t.shape[1] // width
    send_feats, side = pl.pallas_call(
        lay_out,
        in_specs=[pl.BlockSpec(memory_space=pltpu.SMEM)]
        + [pl.BlockSpec(memory_space=pltpu.VMEM)] * 5,
        out_specs=[pl.BlockSpec(memory_space=pl.ANY), pl.BlockSpec(memory_space=pltpu.VMEM)],
        out_shape=[
            jax.ShapeDtypeStruct((parts, width, rows), BF),
            jax.ShapeDtypeStruct((own_blocks + 1 + slices, width, rows), BF),
        ],
        scratch_shapes=[
            pltpu.VMEM((parts, width, rows), BF),
            pltpu.SemaphoreType.DMA((CHUNKS,)),
        ],
    )(
        second.reshape(1).astype(jnp.int32),
        halo_blocks.T,
        feats_t,
        cot_t,
        self_two_t,
        neigh_two_t,
    )
    halo_feats = lax.all_to_all(send_feats, "dom", 0, 0, tiled=True)
    wanted = lax.dynamic_index_in_dim(halo_blocks, me, 0, keepdims=False)
    is_own = tile_index < own_blocks
    tile_block = wanted[jnp.clip(tile_index - own_blocks, 0, wanted.shape[0] - 1)]
    tile_owner = jnp.clip(tile_block // own_blocks, 0, parts - 1)

    onehot = tile_index[:, :, None] == jnp.arange(own_blocks, dtype=jnp.int32)[None, None, :]
    dense = jnp.sum(
        jnp.where(onehot[:, :, :, None, None], tile_weight[:, :, None].astype(F32), 0.0), axis=1
    )
    dense = dense.transpose(0, 2, 1, 3).reshape(owned, owned).astype(BF)
    row_total = jnp.sum(tile_weight, axis=(1, 3), dtype=F32).reshape(1, owned)
    inverse = 1.0 / row_total

    whole = lax.all_gather(side, "feat", axis=0, tiled=False)
    whole_feats = jnp.concatenate(
        [whole[:, i].reshape(-1, rows) for i in range(own_blocks)], axis=1
    )
    whole_cot = whole[:, own_blocks].reshape(-1, seeds)
    columns = lax.dynamic_index_in_dim(
        whole, own_blocks + 1 + lax.axis_index("feat"), 1, keepdims=False
    ).reshape(-1, 2 * width)

    named = jnp.any(halo_blocks == second, axis=1)[:, None, None]
    history_t, named = lax.optimization_barrier((history.T, named))
    send_history = jnp.where(named, history_t[None, :, rows:], history_t[None, :, :rows])
    send_history, dense, inverse, tile_owner, is_own, halo_feats = lax.optimization_barrier(
        (send_history, dense, inverse, tile_owner, is_own, halo_feats)
    )
    halo_history = lax.all_to_all(send_history, "dom", 0, 0, tiled=True)

    def halo_sum(picked):
        picked = jnp.where(is_own[:, :, None, None], jnp.zeros((), BF), picked)
        out = jnp.einsum("bkfc,bkvc->fbv", picked, tile_weight, preferred_element_type=F32)
        return out.reshape(width, owned)

    mean_one = (halo_sum(halo_feats[tile_owner]) + mm(feats_t, dense, ((1,), (1,)))) * inverse
    whole_mean_one = lax.all_gather(mean_one.astype(BF), "feat", axis=0, tiled=True)
    pre_one = mm(self_one_t, whole_feats, ((1,), (0,))) + mm(
        neigh_one_t, whole_mean_one, ((1,), (0,))
    )
    gate = jax.nn.sigmoid(pre_one)
    hidden = (pre_one * gate).astype(BF)

    seed_rows = (
        batch_ids[:, None] == jnp.arange(owned, dtype=jnp.int32)[None, :]
    ).astype(BF)
    whole_grad_two = mm(whole_cot, seed_rows, ((1,), (0,))).astype(BF)
    back = mm(columns, whole_grad_two, ((0,), (0,)))
    scaled = (back[width:] * inverse).astype(BF)
    own_grad = mm(scaled, dense, ((1,), (0,)))
    slope = gate * (1.0 + pre_one * (1.0 - gate))
    grad_one = ((back[:width] + own_grad) * slope).astype(BF)
    ones = mm(
        grad_one, jnp.concatenate([whole_feats, whole_mean_one], axis=0), ((1,), (1,))
    )
    depth = self_one.shape[0]
    lanes = 2 * width
    high = parts * lanes // (2 * depth)
    low = width // high
    ones = ones.astype(BF).reshape(high, low, 2 * depth // lanes, lanes).transpose(0, 2, 1, 3)
    ones = ones.reshape(parts, 1, low, lanes)

    halo_history, ones, hidden, whole_grad_two = lax.optimization_barrier(
        (halo_history, ones, hidden, whole_grad_two)
    )
    mean_two = (
        (halo_sum(halo_history[tile_owner]) + mm(hidden, dense, ((1,), (1,)))) * inverse
    ).astype(BF)
    layer_two = jnp.concatenate([hidden, mean_two], axis=0)

    twos = mm(whole_grad_two, layer_two, ((1,), (1,))).astype(BF)
    twos = lax.all_to_all(twos.reshape(slices, width, 2 * width), "feat", 0, 0, tiled=True)
    layer_two, twos = lax.optimization_barrier((layer_two, twos))
    whole_two = lax.all_gather(layer_two, "feat", axis=0, tiled=False)
    pieces = jnp.concatenate([ones, twos.reshape(parts, 1, low, lanes)], axis=1)
    pieces = with_layout_constraint(pieces, Layout(major_to_minor=(0, 1, 2, 3)))
    got = lax.all_to_all(pieces, "dom", 0, 0, tiled=True)
    mine = jnp.sum(got.astype(F32), axis=0, keepdims=True).astype(BF)
    spread = jnp.broadcast_to(mine, pieces.shape)
    sums = lax.all_to_all(spread, "dom", 0, 0, tiled=True)
    grads = pl.pallas_call(
        unpack,
        in_specs=[pl.BlockSpec(memory_space=pl.ANY)],
        out_shape=[jax.ShapeDtypeStruct((width, depth), F32)] * 4,
        scratch_shapes=[pltpu.VMEM(sums.shape, BF)],
    )(sums)

    whole_hidden = whole_two[:, :width].reshape(depth, owned)
    whole_mean_two = whole_two[:, width:].reshape(depth, owned)
    node_out = mm(self_two_t, whole_hidden, ((1,), (0,))) + mm(
        neigh_two_t, whole_mean_two, ((1,), (0,))
    )
    return (node_out.astype(BF).T, *[grad.T for grad in grads])


def solution(mesh):
    return jax.shard_map(
        on_device,
        mesh=mesh,
        in_specs=(
            P("dom", "feat"),
            P("dom", "feat"),
            P(),
            P("dom", None),
            P("dom", None, None, None),
            P(None, "feat"),
            P(None, "feat"),
            P(None, "feat"),
            P(None, "feat"),
            P("dom"),
            P("dom", "feat"),
        ),
        out_specs=(
            P("dom", "feat"),
            P(None, "feat"),
            P(None, "feat"),
            P(None, "feat"),
            P(None, "feat"),
        ),
        check_vma=False,
    )
```

```python
import jax
import jax.numpy as jnp
from jax import lax
from jax.experimental import pallas as pl
from jax.experimental.pallas import tpu as pltpu
from jax.experimental.layout import Layout, with_layout_constraint
from jax.sharding import PartitionSpec as P

BF = jnp.bfloat16
F32 = jnp.float32


def mm(a, b, dims):
    return lax.dot_general(a, b, (dims, ((), ())), preferred_element_type=F32)


CHUNKS = 4


def lay_out(
    second_ref, halo_ref, rows_ref, seeds_ref, self_ref, neigh_ref, out_ref, side_ref, picked, sems
):
    parts, width, lanes = picked.shape
    names = jnp.where(halo_ref[...] == second_ref[0], 1.0, 0.0)
    names = jnp.max(names, axis=0, keepdims=True)
    names = jnp.broadcast_to(names, (lanes, parts)).T
    low = rows_ref[:, :lanes].astype(F32)
    high = rows_ref[:, lanes:].astype(F32)
    step = parts // CHUNKS
    copies = []
    for chunk in range(CHUNKS):
        for reader in range(chunk * step, (chunk + 1) * step):
            name = jnp.broadcast_to(names[reader : reader + 1, :], low.shape)
            picked[reader] = jnp.where(name > 0.5, high, low).astype(picked.dtype)
        part = pl.ds(chunk * step, step)
        copy = pltpu.make_async_copy(picked.at[part], out_ref.at[part], sems.at[chunk])
        copy.start()
        copies.append(copy)
    side_ref[0] = rows_ref[:, :lanes]
    side_ref[1] = rows_ref[:, lanes:]
    side_ref[2] = seeds_ref[...]
    for pair in range(self_ref.shape[1] // lanes):
        across = slice(pair * lanes, (pair + 1) * lanes)
        own = self_ref[:, across].astype(F32)
        near = neigh_ref[:, across].astype(F32)
        left = jnp.concatenate([own[:, :width], near[:, :width]], axis=1)
        right = jnp.concatenate([own[:, width:], near[:, width:]], axis=1)
        side_ref[3 + 2 * pair] = left.astype(side_ref.dtype)
        side_ref[4 + 2 * pair] = right.astype(side_ref.dtype)
    for copy in copies:
        copy.wait()


def unpack(sums_any, self_one_ref, neigh_one_ref, self_two_ref, neigh_two_ref, sums_ref):
    pltpu.sync_copy(sums_any, sums_ref)
    parts, _, low, lanes = sums_ref.shape
    width, depth = self_one_ref.shape
    high = width // low
    wide = depth // lanes
    for i in range(high):
        down = slice(i * low, (i + 1) * low)
        for j in range(wide):
            across = slice(j * lanes, (j + 1) * lanes)
            base = i * 2 * wide + j
            self_one_ref[down, across] = sums_ref[base, 0].astype(F32)
            neigh_one_ref[down, across] = sums_ref[base + wide, 0].astype(F32)
            left = sums_ref[2 * j * high + i, 1].astype(F32)
            right = sums_ref[(2 * j + 1) * high + i, 1].astype(F32)
            self_two_ref[down, across] = jnp.concatenate(
                [left[:, :width], right[:, :width]], axis=1
            )
            neigh_two_ref[down, across] = jnp.concatenate(
                [left[:, width:], right[:, width:]], axis=1
            )


def on_device(
    node_feats,
    history,
    halo_blocks,
    tile_index,
    tile_weight,
    self_one,
    neigh_one,
    self_two,
    neigh_two,
    batch_ids,
    cotangent,
):
    own_blocks, tiles = tile_index.shape
    rows = tile_weight.shape[2]
    width = node_feats.shape[1]
    owned = node_feats.shape[0]
    parts = halo_blocks.shape[0]
    seeds = cotangent.shape[0]
    me = lax.axis_index("dom")

    feats_t = node_feats.T
    cot_t = cotangent.T
    self_one_t, neigh_one_t, self_two_t, neigh_two_t = (
        self_one.T,
        neigh_one.T,
        self_two.T,
        neigh_two.T,
    )

    second = own_blocks * me + 1
    slices = self_two_t.shape[1] // width
    send_feats, side = pl.pallas_call(
        lay_out,
        in_specs=[pl.BlockSpec(memory_space=pltpu.SMEM)]
        + [pl.BlockSpec(memory_space=pltpu.VMEM)] * 5,
        out_specs=[pl.BlockSpec(memory_space=pl.ANY), pl.BlockSpec(memory_space=pltpu.VMEM)],
        out_shape=[
            jax.ShapeDtypeStruct((parts, width, rows), BF),
            jax.ShapeDtypeStruct((own_blocks + 1 + slices, width, rows), BF),
        ],
        scratch_shapes=[
            pltpu.VMEM((parts, width, rows), BF),
            pltpu.SemaphoreType.DMA((CHUNKS,)),
        ],
    )(
        second.reshape(1).astype(jnp.int32),
        halo_blocks.T,
        feats_t,
        cot_t,
        self_two_t,
        neigh_two_t,
    )
    halo_feats = lax.all_to_all(send_feats, "dom", 0, 0, tiled=True)
    wanted = lax.dynamic_index_in_dim(halo_blocks, me, 0, keepdims=False)
    is_own = tile_index < own_blocks
    tile_block = wanted[jnp.clip(tile_index - own_blocks, 0, wanted.shape[0] - 1)]
    tile_owner = jnp.clip(tile_block // own_blocks, 0, parts - 1)

    onehot = tile_index[:, :, None] == jnp.arange(own_blocks, dtype=jnp.int32)[None, None, :]
    dense = jnp.sum(
        jnp.where(onehot[:, :, :, None, None], tile_weight[:, :, None].astype(F32), 0.0), axis=1
    )
    dense = dense.transpose(0, 2, 1, 3).reshape(owned, owned).astype(BF)
    row_total = jnp.sum(tile_weight, axis=(1, 3), dtype=F32).reshape(1, owned)
    inverse = 1.0 / row_total

    whole = lax.all_gather(side, "feat", axis=0, tiled=False)
    whole_feats = jnp.concatenate(
        [whole[:, i].reshape(-1, rows) for i in range(own_blocks)], axis=1
    )
    whole_cot = whole[:, own_blocks].reshape(-1, seeds)
    columns = lax.dynamic_index_in_dim(
        whole, own_blocks + 1 + lax.axis_index("feat"), 1, keepdims=False
    ).reshape(-1, 2 * width)

    named = jnp.any(halo_blocks == second, axis=1)[:, None, None]
    history_t, named = lax.optimization_barrier((history.T, named))
    send_history = jnp.where(named, history_t[None, :, rows:], history_t[None, :, :rows])
    send_history, dense, inverse, tile_owner, is_own, halo_feats = lax.optimization_barrier(
        (send_history, dense, inverse, tile_owner, is_own, halo_feats)
    )
    halo_history = lax.all_to_all(send_history, "dom", 0, 0, tiled=True)

    def halo_sum(picked):
        picked = jnp.where(is_own[:, :, None, None], jnp.zeros((), BF), picked)
        out = jnp.einsum("bkfc,bkvc->fbv", picked, tile_weight, preferred_element_type=F32)
        return out.reshape(width, owned)

    mean_one = (halo_sum(halo_feats[tile_owner]) + mm(feats_t, dense, ((1,), (1,)))) * inverse
    whole_mean_one = lax.all_gather(mean_one.astype(BF), "feat", axis=0, tiled=True)
    pre_one = mm(self_one_t, whole_feats, ((1,), (0,))) + mm(
        neigh_one_t, whole_mean_one, ((1,), (0,))
    )
    gate = jax.nn.sigmoid(pre_one)
    hidden = (pre_one * gate).astype(BF)

    seed_rows = (
        batch_ids[:, None] == jnp.arange(owned, dtype=jnp.int32)[None, :]
    ).astype(BF)
    whole_grad_two = mm(whole_cot, seed_rows, ((1,), (0,))).astype(BF)

    halo_history, hidden, whole_grad_two = lax.optimization_barrier(
        (halo_history, hidden, whole_grad_two)
    )
    mean_two = (
        (halo_sum(halo_history[tile_owner]) + mm(hidden, dense, ((1,), (1,)))) * inverse
    ).astype(BF)
    layer_two = jnp.concatenate([hidden, mean_two], axis=0)

    twos = mm(whole_grad_two, layer_two, ((1,), (1,))).astype(BF)
    twos, columns, pre_one, gate = lax.optimization_barrier((twos, columns, pre_one, gate))
    back = mm(columns, whole_grad_two, ((0,), (0,)))
    scaled = (back[width:] * inverse).astype(BF)
    own_grad = mm(scaled, dense, ((1,), (0,)))
    slope = gate * (1.0 + pre_one * (1.0 - gate))
    grad_one = ((back[:width] + own_grad) * slope).astype(BF)
    ones = mm(
        grad_one, jnp.concatenate([whole_feats, whole_mean_one], axis=0), ((1,), (1,))
    )
    depth = self_one.shape[0]
    lanes = 2 * width
    high = parts * lanes // (2 * depth)
    low = width // high
    ones = ones.astype(BF).reshape(high, low, 2 * depth // lanes, lanes).transpose(0, 2, 1, 3)
    ones = ones.reshape(parts, 1, low, lanes)
    twos = lax.all_to_all(twos.reshape(slices, width, 2 * width), "feat", 0, 0, tiled=True)
    layer_two, twos, ones = lax.optimization_barrier((layer_two, twos, ones))
    whole_two = lax.all_gather(layer_two, "feat", axis=0, tiled=False)
    pieces = jnp.concatenate([ones, twos.reshape(parts, 1, low, lanes)], axis=1)
    pieces = with_layout_constraint(pieces, Layout(major_to_minor=(0, 1, 2, 3)))
    got = lax.all_to_all(pieces, "dom", 0, 0, tiled=True)
    mine = jnp.sum(got.astype(F32), axis=0, keepdims=True).astype(BF)
    spread = jnp.broadcast_to(mine, pieces.shape)
    sums = lax.all_to_all(spread, "dom", 0, 0, tiled=True)
    grads = pl.pallas_call(
        unpack,
        in_specs=[pl.BlockSpec(memory_space=pl.ANY)],
        out_shape=[jax.ShapeDtypeStruct((width, depth), F32)] * 4,
        scratch_shapes=[pltpu.VMEM(sums.shape, BF)],
        compiler_params=pltpu.CompilerParams(vmem_limit_bytes=6 << 20),
    )(sums)

    whole_hidden = whole_two[:, :width].reshape(depth, owned)
    whole_mean_two = whole_two[:, width:].reshape(depth, owned)
    node_out = mm(self_two_t, whole_hidden, ((1,), (0,))) + mm(
        neigh_two_t, whole_mean_two, ((1,), (0,))
    )
    return (node_out.astype(BF).T, *[grad.T for grad in grads])


def solution(mesh):
    return jax.shard_map(
        on_device,
        mesh=mesh,
        in_specs=(
            P("dom", "feat"),
            P("dom", "feat"),
            P(),
            P("dom", None),
            P("dom", None, None, None),
            P(None, "feat"),
            P(None, "feat"),
            P(None, "feat"),
            P(None, "feat"),
            P("dom"),
            P("dom", "feat"),
        ),
        out_specs=(
            P("dom", "feat"),
            P(None, "feat"),
            P(None, "feat"),
            P(None, "feat"),
            P(None, "feat"),
        ),
        check_vma=False,
    )
```

```python
import jax
import jax.numpy as jnp
from jax import lax
from jax.experimental import pallas as pl
from jax.experimental.pallas import tpu as pltpu
from jax.experimental.layout import Layout, with_layout_constraint
from jax.sharding import PartitionSpec as P

BF = jnp.bfloat16
F32 = jnp.float32


def mm(a, b, dims):
    return lax.dot_general(a, b, (dims, ((), ())), preferred_element_type=F32)


CHUNKS = 4


def lay_out(
    second_ref, halo_ref, rows_ref, seeds_ref, self_ref, neigh_ref, out_ref, side_ref, picked, sems
):
    parts, width, lanes = picked.shape
    names = jnp.where(halo_ref[...] == second_ref[0], 1.0, 0.0)
    names = jnp.max(names, axis=0, keepdims=True)
    names = jnp.broadcast_to(names, (lanes, parts)).T
    low = rows_ref[:, :lanes].astype(F32)
    high = rows_ref[:, lanes:].astype(F32)
    step = parts // CHUNKS
    copies = []
    for chunk in range(CHUNKS):
        for reader in range(chunk * step, (chunk + 1) * step):
            name = jnp.broadcast_to(names[reader : reader + 1, :], low.shape)
            picked[reader] = jnp.where(name > 0.5, high, low).astype(picked.dtype)
        part = pl.ds(chunk * step, step)
        copy = pltpu.make_async_copy(picked.at[part], out_ref.at[part], sems.at[chunk])
        copy.start()
        copies.append(copy)
    side_ref[0] = rows_ref[:, :lanes]
    side_ref[1] = rows_ref[:, lanes:]
    side_ref[2] = seeds_ref[...]
    for pair in range(self_ref.shape[1] // lanes):
        across = slice(pair * lanes, (pair + 1) * lanes)
        own = self_ref[:, across].astype(F32)
        near = neigh_ref[:, across].astype(F32)
        left = jnp.concatenate([own[:, :width], near[:, :width]], axis=1)
        right = jnp.concatenate([own[:, width:], near[:, width:]], axis=1)
        side_ref[3 + 2 * pair] = left.astype(side_ref.dtype)
        side_ref[4 + 2 * pair] = right.astype(side_ref.dtype)
    for copy in copies:
        copy.wait()


def unpack(sums_any, self_one_ref, neigh_one_ref, self_two_ref, neigh_two_ref, sums_ref):
    pltpu.sync_copy(sums_any, sums_ref)
    parts, _, low, lanes = sums_ref.shape
    width, depth = self_one_ref.shape
    high = width // low
    wide = depth // lanes
    for i in range(high):
        down = slice(i * low, (i + 1) * low)
        for j in range(wide):
            across = slice(j * lanes, (j + 1) * lanes)
            base = i * 2 * wide + j
            self_one_ref[down, across] = sums_ref[base, 0].astype(F32)
            neigh_one_ref[down, across] = sums_ref[base + wide, 0].astype(F32)
            left = sums_ref[2 * j * high + i, 1].astype(F32)
            right = sums_ref[(2 * j + 1) * high + i, 1].astype(F32)
            self_two_ref[down, across] = jnp.concatenate(
                [left[:, :width], right[:, :width]], axis=1
            )
            neigh_two_ref[down, across] = jnp.concatenate(
                [left[:, width:], right[:, width:]], axis=1
            )


def on_device(
    node_feats,
    history,
    halo_blocks,
    tile_index,
    tile_weight,
    self_one,
    neigh_one,
    self_two,
    neigh_two,
    batch_ids,
    cotangent,
):
    own_blocks, tiles = tile_index.shape
    rows = tile_weight.shape[2]
    width = node_feats.shape[1]
    owned = node_feats.shape[0]
    parts = halo_blocks.shape[0]
    seeds = cotangent.shape[0]
    me = lax.axis_index("dom")

    feats_t = node_feats.T
    cot_t = cotangent.T
    self_one_t, neigh_one_t, self_two_t, neigh_two_t = (
        self_one.T,
        neigh_one.T,
        self_two.T,
        neigh_two.T,
    )

    second = own_blocks * me + 1
    slices = self_two_t.shape[1] // width
    send_feats, side = pl.pallas_call(
        lay_out,
        in_specs=[pl.BlockSpec(memory_space=pltpu.SMEM)]
        + [pl.BlockSpec(memory_space=pltpu.VMEM)] * 5,
        out_specs=[pl.BlockSpec(memory_space=pl.ANY), pl.BlockSpec(memory_space=pltpu.VMEM)],
        out_shape=[
            jax.ShapeDtypeStruct((parts, width, rows), BF),
            jax.ShapeDtypeStruct((own_blocks + 1 + slices, width, rows), BF),
        ],
        scratch_shapes=[
            pltpu.VMEM((parts, width, rows), BF),
            pltpu.SemaphoreType.DMA((CHUNKS,)),
        ],
    )(
        second.reshape(1).astype(jnp.int32),
        halo_blocks.T,
        feats_t,
        cot_t,
        self_two_t,
        neigh_two_t,
    )
    halo_feats = lax.all_to_all(send_feats, "dom", 0, 0, tiled=True)
    wanted = lax.dynamic_index_in_dim(halo_blocks, me, 0, keepdims=False)
    is_own = tile_index < own_blocks
    tile_block = wanted[jnp.clip(tile_index - own_blocks, 0, wanted.shape[0] - 1)]
    tile_owner = jnp.clip(tile_block // own_blocks, 0, parts - 1)

    onehot = tile_index[:, :, None] == jnp.arange(own_blocks, dtype=jnp.int32)[None, None, :]
    dense = jnp.sum(
        jnp.where(onehot[:, :, :, None, None], tile_weight[:, :, None].astype(F32), 0.0), axis=1
    )
    dense = dense.transpose(0, 2, 1, 3).reshape(owned, owned).astype(BF)
    row_total = jnp.sum(tile_weight, axis=(1, 3), dtype=F32).reshape(1, owned)
    inverse = 1.0 / row_total

    whole = lax.all_gather(side, "feat", axis=0, tiled=False)
    whole_feats = jnp.concatenate(
        [whole[:, i].reshape(-1, rows) for i in range(own_blocks)], axis=1
    )
    whole_cot = whole[:, own_blocks].reshape(-1, seeds)
    columns = lax.dynamic_index_in_dim(
        whole, own_blocks + 1 + lax.axis_index("feat"), 1, keepdims=False
    ).reshape(-1, 2 * width)

    named = jnp.any(halo_blocks == second, axis=1)[:, None, None]
    history_t, named = lax.optimization_barrier((history.T, named))
    send_history = jnp.where(named, history_t[None, :, rows:], history_t[None, :, :rows])
    send_history, dense, inverse, tile_owner, is_own, halo_feats = lax.optimization_barrier(
        (send_history, dense, inverse, tile_owner, is_own, halo_feats)
    )
    halo_history = lax.all_to_all(send_history, "dom", 0, 0, tiled=True)

    def halo_sum(picked):
        picked = jnp.where(is_own[:, :, None, None], jnp.zeros((), BF), picked)
        out = jnp.einsum("bkfc,bkvc->fbv", picked, tile_weight, preferred_element_type=F32)
        return out.reshape(width, owned)

    mean_one = (halo_sum(halo_feats[tile_owner]) + mm(feats_t, dense, ((1,), (1,)))) * inverse
    whole_mean_one = lax.all_gather(mean_one.astype(BF), "feat", axis=0, tiled=True)
    pre_one = mm(self_one_t, whole_feats, ((1,), (0,))) + mm(
        neigh_one_t, whole_mean_one, ((1,), (0,))
    )
    gate = jax.nn.sigmoid(pre_one)
    hidden = (pre_one * gate).astype(BF)

    seed_rows = (
        batch_ids[:, None] == jnp.arange(owned, dtype=jnp.int32)[None, :]
    ).astype(BF)
    whole_grad_two = mm(whole_cot, seed_rows, ((1,), (0,))).astype(BF)

    back = mm(columns, whole_grad_two, ((0,), (0,)))
    scaled = (back[width:] * inverse).astype(BF)
    own_grad = mm(scaled, dense, ((1,), (0,)))
    slope = gate * (1.0 + pre_one * (1.0 - gate))
    grad_one = ((back[:width] + own_grad) * slope).astype(BF)
    ones = mm(
        grad_one, jnp.concatenate([whole_feats, whole_mean_one], axis=0), ((1,), (1,))
    )
    depth = self_one.shape[0]
    lanes = 2 * width
    high = parts * lanes // (2 * depth)
    low = width // high
    ones = ones.astype(BF).reshape(high, low, 2 * depth // lanes, lanes).transpose(0, 2, 1, 3)
    ones = ones.reshape(parts, 1, low, lanes)

    halo_history, ones, hidden, whole_grad_two = lax.optimization_barrier(
        (halo_history, ones, hidden, whole_grad_two)
    )
    mean_two = (
        (halo_sum(halo_history[tile_owner]) + mm(hidden, dense, ((1,), (1,)))) * inverse
    ).astype(BF)
    layer_two = jnp.concatenate([hidden, mean_two], axis=0)

    twos = mm(whole_grad_two, layer_two, ((1,), (1,))).astype(BF)
    twos, layer_two, ones = lax.optimization_barrier((twos, layer_two, ones))
    twos = lax.all_to_all(twos.reshape(slices, width, 2 * width), "feat", 0, 0, tiled=True)
    layer_two, twos, ones = lax.optimization_barrier((layer_two, twos, ones))
    whole_two = lax.all_gather(layer_two, "feat", axis=0, tiled=False)
    pieces = jnp.concatenate([ones, twos.reshape(parts, 1, low, lanes)], axis=1)
    pieces = with_layout_constraint(pieces, Layout(major_to_minor=(0, 1, 2, 3)))
    got = lax.all_to_all(pieces, "dom", 0, 0, tiled=True)
    mine = jnp.sum(got.astype(F32), axis=0, keepdims=True).astype(BF)
    spread = jnp.broadcast_to(mine, pieces.shape)
    sums = lax.all_to_all(spread, "dom", 0, 0, tiled=True)
    grads = pl.pallas_call(
        unpack,
        in_specs=[pl.BlockSpec(memory_space=pl.ANY)],
        out_shape=[jax.ShapeDtypeStruct((width, depth), F32)] * 4,
        scratch_shapes=[pltpu.VMEM(sums.shape, BF)],
        compiler_params=pltpu.CompilerParams(vmem_limit_bytes=6 << 20),
    )(sums)

    whole_hidden = whole_two[:, :width].reshape(depth, owned)
    whole_mean_two = whole_two[:, width:].reshape(depth, owned)
    node_out = mm(self_two_t, whole_hidden, ((1,), (0,))) + mm(
        neigh_two_t, whole_mean_two, ((1,), (0,))
    )
    return (node_out.astype(BF).T, *[grad.T for grad in grads])


def solution(mesh):
    return jax.shard_map(
        on_device,
        mesh=mesh,
        in_specs=(
            P("dom", "feat"),
            P("dom", "feat"),
            P(),
            P("dom", None),
            P("dom", None, None, None),
            P(None, "feat"),
            P(None, "feat"),
            P(None, "feat"),
            P(None, "feat"),
            P("dom"),
            P("dom", "feat"),
        ),
        out_specs=(
            P("dom", "feat"),
            P(None, "feat"),
            P(None, "feat"),
            P(None, "feat"),
            P(None, "feat"),
        ),
        check_vma=False,
    )
```

```python
import jax
import jax.numpy as jnp
from jax import lax
from jax.experimental import pallas as pl
from jax.experimental.pallas import tpu as pltpu
from jax.experimental.layout import Layout, with_layout_constraint
from jax.sharding import PartitionSpec as P

BF = jnp.bfloat16
F32 = jnp.float32


def mm(a, b, dims):
    return lax.dot_general(a, b, (dims, ((), ())), preferred_element_type=F32)


CHUNKS = 4


def lay_out(
    me_ref,
    halo_any,
    rows_any,
    seeds_any,
    self_any,
    neigh_any,
    out_any,
    side_any,
    halo_ref,
    rows_ref,
    seeds_ref,
    self_ref,
    neigh_ref,
    picked,
    side_ref,
    in_sems,
    out_sems,
):
    def fetch(source, target, index):
        copy = pltpu.make_async_copy(source, target, in_sems.at[index])
        copy.start()
        return copy

    get_halo = fetch(halo_any, halo_ref, 0)
    get_rows = fetch(rows_any, rows_ref, 1)
    get_seeds = fetch(seeds_any, seeds_ref, 2)
    get_self = fetch(self_any, self_ref, 3)
    get_neigh = fetch(neigh_any, neigh_ref, 4)
    parts, width, lanes = picked.shape
    get_halo.wait()
    names = jnp.where(halo_ref[...] == 2 * me_ref[0] + 1, 1.0, 0.0)
    names = jnp.max(names, axis=0, keepdims=True)
    readers = lax.broadcasted_iota(jnp.int32, (1, parts), 1)
    names = jnp.where(readers == me_ref[0], 2.0, names)
    names = jnp.broadcast_to(names, (lanes, parts)).T
    get_rows.wait()
    low = rows_ref[:, :lanes].astype(F32)
    high = rows_ref[:, lanes:].astype(F32)
    step = parts // CHUNKS
    copies = []
    for chunk in range(CHUNKS):
        for reader in range(chunk * step, (chunk + 1) * step):
            name = jnp.broadcast_to(names[reader : reader + 1, :], low.shape)
            block = jnp.where(name > 1.5, 0.0, jnp.where(name > 0.5, high, low))
            picked[reader] = block.astype(picked.dtype)
        part = pl.ds(chunk * step, step)
        copy = pltpu.make_async_copy(picked.at[part], out_any.at[part], out_sems.at[chunk])
        copy.start()
        copies.append(copy)
    side_ref[0] = rows_ref[:, :lanes]
    side_ref[1] = rows_ref[:, lanes:]
    get_seeds.wait()
    side_ref[2] = seeds_ref[...]
    get_self.wait()
    get_neigh.wait()
    for pair in range(self_ref.shape[1] // lanes):
        across = slice(pair * lanes, (pair + 1) * lanes)
        own = self_ref[:, across].astype(F32)
        near = neigh_ref[:, across].astype(F32)
        left = jnp.concatenate([own[:, :width], near[:, :width]], axis=1)
        right = jnp.concatenate([own[:, width:], near[:, width:]], axis=1)
        side_ref[3 + 2 * pair] = left.astype(side_ref.dtype)
        side_ref[4 + 2 * pair] = right.astype(side_ref.dtype)
    copy = pltpu.make_async_copy(side_ref, side_any, out_sems.at[CHUNKS])
    copy.start()
    copies.append(copy)
    for copy in copies:
        copy.wait()


def unpack(sums_any, self_one_ref, neigh_one_ref, self_two_ref, neigh_two_ref, sums_ref):
    pltpu.sync_copy(sums_any, sums_ref)
    parts, _, low, lanes = sums_ref.shape
    width, depth = self_one_ref.shape
    high = width // low
    wide = depth // lanes
    for i in range(high):
        down = slice(i * low, (i + 1) * low)
        for j in range(wide):
            across = slice(j * lanes, (j + 1) * lanes)
            base = i * 2 * wide + j
            self_one_ref[down, across] = sums_ref[base, 0].astype(F32)
            neigh_one_ref[down, across] = sums_ref[base + wide, 0].astype(F32)
            left = sums_ref[2 * j * high + i, 1].astype(F32)
            right = sums_ref[(2 * j + 1) * high + i, 1].astype(F32)
            self_two_ref[down, across] = jnp.concatenate(
                [left[:, :width], right[:, :width]], axis=1
            )
            neigh_two_ref[down, across] = jnp.concatenate(
                [left[:, width:], right[:, width:]], axis=1
            )


def on_device(
    node_feats,
    history,
    halo_blocks,
    tile_index,
    tile_weight,
    self_one,
    neigh_one,
    self_two,
    neigh_two,
    batch_ids,
    cotangent,
):
    own_blocks, tiles = tile_index.shape
    rows = tile_weight.shape[2]
    width = node_feats.shape[1]
    owned = node_feats.shape[0]
    parts = halo_blocks.shape[0]
    seeds = cotangent.shape[0]
    me = lax.axis_index("dom")

    feats_t = node_feats.T
    cot_t = cotangent.T
    self_one_t, neigh_one_t, self_two_t, neigh_two_t = (
        self_one.T,
        neigh_one.T,
        self_two.T,
        neigh_two.T,
    )

    second = own_blocks * me + 1
    slices = self_two_t.shape[1] // width
    side_shape = (own_blocks + 1 + slices, width, rows)
    operands = (halo_blocks.T, feats_t, cot_t, self_two_t, neigh_two_t)
    send_feats, side = pl.pallas_call(
        lay_out,
        in_specs=[pl.BlockSpec(memory_space=pltpu.SMEM)]
        + [pl.BlockSpec(memory_space=pl.ANY)] * len(operands),
        out_specs=[pl.BlockSpec(memory_space=pl.ANY)] * 2,
        out_shape=[
            jax.ShapeDtypeStruct((parts, width, rows), BF),
            jax.ShapeDtypeStruct(side_shape, BF),
        ],
        scratch_shapes=[pltpu.VMEM(operand.shape, operand.dtype) for operand in operands]
        + [
            pltpu.VMEM((parts, width, rows), BF),
            pltpu.VMEM(side_shape, BF),
            pltpu.SemaphoreType.DMA((len(operands),)),
            pltpu.SemaphoreType.DMA((CHUNKS + 1,)),
        ],
    )(me.reshape(1).astype(jnp.int32), *operands)
    halo_feats = lax.all_to_all(send_feats, "dom", 0, 0, tiled=True)
    wanted = lax.dynamic_index_in_dim(halo_blocks, me, 0, keepdims=False)
    is_own = tile_index < own_blocks
    tile_block = wanted[jnp.clip(tile_index - own_blocks, 0, wanted.shape[0] - 1)]
    tile_slot = jnp.where(is_own, me, jnp.clip(tile_block // own_blocks, 0, parts - 1))

    onehot = tile_index[:, :, None] == jnp.arange(own_blocks, dtype=jnp.int32)[None, None, :]
    dense = jnp.sum(
        jnp.where(onehot[:, :, :, None, None], tile_weight[:, :, None].astype(F32), 0.0), axis=1
    )
    dense = dense.transpose(0, 2, 1, 3).reshape(owned, owned).astype(BF)
    row_total = jnp.sum(tile_weight, axis=(1, 3), dtype=F32).reshape(1, owned)
    inverse = 1.0 / row_total

    whole = lax.all_gather(side, "feat", axis=0, tiled=False)
    whole_feats = jnp.concatenate(
        [whole[:, i].reshape(-1, rows) for i in range(own_blocks)], axis=1
    )
    whole_cot = whole[:, own_blocks].reshape(-1, seeds)
    columns = lax.dynamic_index_in_dim(
        whole, own_blocks + 1 + lax.axis_index("feat"), 1, keepdims=False
    ).reshape(-1, 2 * width)

    named = jnp.any(halo_blocks == second, axis=1).astype(jnp.int32)
    named = jnp.where(jnp.arange(parts, dtype=jnp.int32) == me, 2, named)[:, None, None]
    history_t, named = lax.optimization_barrier((history.T, named))
    send_history = jnp.where(named == 1, history_t[None, :, rows:], history_t[None, :, :rows])
    send_history = jnp.where(named == 2, jnp.zeros((), BF), send_history)
    send_history, dense, inverse, tile_slot, halo_feats = lax.optimization_barrier(
        (send_history, dense, inverse, tile_slot, halo_feats)
    )
    halo_history = lax.all_to_all(send_history, "dom", 0, 0, tiled=True)

    def halo_sum(picked):
        out = jnp.einsum("bkfc,bkvc->fbv", picked, tile_weight, preferred_element_type=F32)
        return out.reshape(width, owned)

    mean_one = (halo_sum(halo_feats[tile_slot]) + mm(feats_t, dense, ((1,), (1,)))) * inverse
    whole_mean_one = lax.all_gather(mean_one.astype(BF), "feat", axis=0, tiled=True)
    pre_one = mm(self_one_t, whole_feats, ((1,), (0,))) + mm(
        neigh_one_t, whole_mean_one, ((1,), (0,))
    )
    gate = jax.nn.sigmoid(pre_one)
    hidden = (pre_one * gate).astype(BF)

    seed_rows = (
        batch_ids[:, None] == jnp.arange(owned, dtype=jnp.int32)[None, :]
    ).astype(BF)
    whole_grad_two = mm(whole_cot, seed_rows, ((1,), (0,))).astype(BF)

    halo_history, hidden, whole_grad_two = lax.optimization_barrier(
        (halo_history, hidden, whole_grad_two)
    )
    mean_two = (
        (halo_sum(halo_history[tile_slot]) + mm(hidden, dense, ((1,), (1,)))) * inverse
    ).astype(BF)
    layer_two = jnp.concatenate([hidden, mean_two], axis=0)

    twos = mm(whole_grad_two, layer_two, ((1,), (1,))).astype(BF)
    twos, columns, pre_one, gate = lax.optimization_barrier((twos, columns, pre_one, gate))
    back = mm(columns, whole_grad_two, ((0,), (0,)))
    scaled = (back[width:] * inverse).astype(BF)
    own_grad = mm(scaled, dense, ((1,), (0,)))
    slope = gate * (1.0 + pre_one * (1.0 - gate))
    grad_one = ((back[:width] + own_grad) * slope).astype(BF)
    ones = mm(
        grad_one, jnp.concatenate([whole_feats, whole_mean_one], axis=0), ((1,), (1,))
    )
    depth = self_one.shape[0]
    lanes = 2 * width
    high = parts * lanes // (2 * depth)
    low = width // high
    ones = ones.astype(BF).reshape(high, low, 2 * depth // lanes, lanes).transpose(0, 2, 1, 3)
    ones = ones.reshape(parts, 1, low, lanes)
    twos = lax.all_to_all(twos.reshape(slices, width, 2 * width), "feat", 0, 0, tiled=True)
    layer_two, twos, ones = lax.optimization_barrier((layer_two, twos, ones))
    whole_two = lax.all_gather(layer_two, "feat", axis=0, tiled=False)
    pieces = jnp.concatenate([ones, twos.reshape(parts, 1, low, lanes)], axis=1)
    pieces = with_layout_constraint(pieces, Layout(major_to_minor=(0, 1, 2, 3)))
    got = lax.all_to_all(pieces, "dom", 0, 0, tiled=True)
    mine = jnp.sum(got.astype(F32), axis=0, keepdims=True).astype(BF)
    spread = jnp.broadcast_to(mine, pieces.shape)
    sums = lax.all_to_all(spread, "dom", 0, 0, tiled=True)
    grads = pl.pallas_call(
        unpack,
        in_specs=[pl.BlockSpec(memory_space=pl.ANY)],
        out_shape=[jax.ShapeDtypeStruct((width, depth), F32)] * 4,
        scratch_shapes=[pltpu.VMEM(sums.shape, BF)],
        compiler_params=pltpu.CompilerParams(vmem_limit_bytes=6 << 20),
    )(sums)

    whole_hidden = whole_two[:, :width].reshape(depth, owned)
    whole_mean_two = whole_two[:, width:].reshape(depth, owned)
    node_out = mm(self_two_t, whole_hidden, ((1,), (0,))) + mm(
        neigh_two_t, whole_mean_two, ((1,), (0,))
    )
    return (node_out.astype(BF).T, *[grad.T for grad in grads])


def solution(mesh):
    return jax.shard_map(
        on_device,
        mesh=mesh,
        in_specs=(
            P("dom", "feat"),
            P("dom", "feat"),
            P(),
            P("dom", None),
            P("dom", None, None, None),
            P(None, "feat"),
            P(None, "feat"),
            P(None, "feat"),
            P(None, "feat"),
            P("dom"),
            P("dom", "feat"),
        ),
        out_specs=(
            P("dom", "feat"),
            P(None, "feat"),
            P(None, "feat"),
            P(None, "feat"),
            P(None, "feat"),
        ),
        check_vma=False,
    )
```

```python
import jax
import jax.numpy as jnp
from jax import lax
from jax.experimental import pallas as pl
from jax.experimental.pallas import tpu as pltpu
from jax.experimental.layout import Layout, with_layout_constraint
from jax.sharding import PartitionSpec as P

BF = jnp.bfloat16
F32 = jnp.float32


def mm(a, b, dims):
    return lax.dot_general(a, b, (dims, ((), ())), preferred_element_type=F32)


CHUNKS = 4
SIDE = 8
MEMBERS = [(r % SIDE) * SIDE + (r // SIDE + r) % SIDE for r in range(SIDE * SIDE)]


def member_of(partition):
    first, second = partition // SIDE, partition % SIDE
    return (second - first + SIDE) % SIDE * SIDE + first


def exchange(pieces):
    return lax.all_to_all(pieces, "dom", 0, 0, axis_index_groups=[MEMBERS], tiled=True)


def lay_out(
    me_ref,
    halo_any,
    rows_any,
    seeds_any,
    self_any,
    neigh_any,
    out_any,
    side_any,
    halo_ref,
    rows_ref,
    seeds_ref,
    self_ref,
    neigh_ref,
    picked,
    side_ref,
    in_sems,
    out_sems,
):
    def fetch(source, target, index):
        copy = pltpu.make_async_copy(source, target, in_sems.at[index])
        copy.start()
        return copy

    get_halo = fetch(halo_any, halo_ref, 0)
    get_rows = fetch(rows_any, rows_ref, 1)
    get_seeds = fetch(seeds_any, seeds_ref, 2)
    get_self = fetch(self_any, self_ref, 3)
    get_neigh = fetch(neigh_any, neigh_ref, 4)
    parts, width, lanes = picked.shape
    get_halo.wait()
    names = jnp.where(halo_ref[...] == 2 * me_ref[0] + 1, 1.0, 0.0)
    names = jnp.max(names, axis=0, keepdims=True)
    readers = lax.broadcasted_iota(jnp.int32, (1, parts), 1)
    names = jnp.where(readers == me_ref[0], 2.0, names)
    names = jnp.broadcast_to(names, (lanes, parts)).T
    get_rows.wait()
    low = rows_ref[:, :lanes].astype(F32)
    high = rows_ref[:, lanes:].astype(F32)
    step = parts // CHUNKS
    copies = []
    for chunk in range(CHUNKS):
        for reader in range(chunk * step, (chunk + 1) * step):
            named = MEMBERS[reader]
            name = jnp.broadcast_to(names[named : named + 1, :], low.shape)
            block = jnp.where(name > 1.5, 0.0, jnp.where(name > 0.5, high, low))
            picked[reader] = block.astype(picked.dtype)
        part = pl.ds(chunk * step, step)
        copy = pltpu.make_async_copy(picked.at[part], out_any.at[part], out_sems.at[chunk])
        copy.start()
        copies.append(copy)
    side_ref[0] = rows_ref[:, :lanes]
    side_ref[1] = rows_ref[:, lanes:]
    get_seeds.wait()
    side_ref[2] = seeds_ref[...]
    get_self.wait()
    get_neigh.wait()
    for pair in range(self_ref.shape[1] // lanes):
        across = slice(pair * lanes, (pair + 1) * lanes)
        own = self_ref[:, across].astype(F32)
        near = neigh_ref[:, across].astype(F32)
        left = jnp.concatenate([own[:, :width], near[:, :width]], axis=1)
        right = jnp.concatenate([own[:, width:], near[:, width:]], axis=1)
        side_ref[3 + 2 * pair] = left.astype(side_ref.dtype)
        side_ref[4 + 2 * pair] = right.astype(side_ref.dtype)
    copy = pltpu.make_async_copy(side_ref, side_any, out_sems.at[CHUNKS])
    copy.start()
    copies.append(copy)
    for copy in copies:
        copy.wait()


def unpack(sums_any, self_one_ref, neigh_one_ref, self_two_ref, neigh_two_ref, sums_ref):
    pltpu.sync_copy(sums_any, sums_ref)
    parts, _, low, lanes = sums_ref.shape
    width, depth = self_one_ref.shape
    high = width // low
    wide = depth // lanes
    for i in range(high):
        down = slice(i * low, (i + 1) * low)
        for j in range(wide):
            across = slice(j * lanes, (j + 1) * lanes)
            base = i * 2 * wide + j
            self_one_ref[down, across] = sums_ref[base, 0].astype(F32)
            neigh_one_ref[down, across] = sums_ref[base + wide, 0].astype(F32)
            left = sums_ref[2 * j * high + i, 1].astype(F32)
            right = sums_ref[(2 * j + 1) * high + i, 1].astype(F32)
            self_two_ref[down, across] = jnp.concatenate(
                [left[:, :width], right[:, :width]], axis=1
            )
            neigh_two_ref[down, across] = jnp.concatenate(
                [left[:, width:], right[:, width:]], axis=1
            )


def on_device(
    node_feats,
    history,
    halo_blocks,
    tile_index,
    tile_weight,
    self_one,
    neigh_one,
    self_two,
    neigh_two,
    batch_ids,
    cotangent,
):
    own_blocks, tiles = tile_index.shape
    rows = tile_weight.shape[2]
    width = node_feats.shape[1]
    owned = node_feats.shape[0]
    parts = halo_blocks.shape[0]
    seeds = cotangent.shape[0]
    me = lax.axis_index("dom")

    feats_t = node_feats.T
    cot_t = cotangent.T
    self_one_t, neigh_one_t, self_two_t, neigh_two_t = (
        self_one.T,
        neigh_one.T,
        self_two.T,
        neigh_two.T,
    )

    second = own_blocks * me + 1
    slices = self_two_t.shape[1] // width
    side_shape = (own_blocks + 1 + slices, width, rows)
    operands = (halo_blocks.T, feats_t, cot_t, self_two_t, neigh_two_t)
    send_feats, side = pl.pallas_call(
        lay_out,
        in_specs=[pl.BlockSpec(memory_space=pltpu.SMEM)]
        + [pl.BlockSpec(memory_space=pl.ANY)] * len(operands),
        out_specs=[pl.BlockSpec(memory_space=pl.ANY)] * 2,
        out_shape=[
            jax.ShapeDtypeStruct((parts, width, rows), BF),
            jax.ShapeDtypeStruct(side_shape, BF),
        ],
        scratch_shapes=[pltpu.VMEM(operand.shape, operand.dtype) for operand in operands]
        + [
            pltpu.VMEM((parts, width, rows), BF),
            pltpu.VMEM(side_shape, BF),
            pltpu.SemaphoreType.DMA((len(operands),)),
            pltpu.SemaphoreType.DMA((CHUNKS + 1,)),
        ],
    )(me.reshape(1).astype(jnp.int32), *operands)
    halo_feats = exchange(send_feats)
    wanted = lax.dynamic_index_in_dim(halo_blocks, me, 0, keepdims=False)
    is_own = tile_index < own_blocks
    tile_block = wanted[jnp.clip(tile_index - own_blocks, 0, wanted.shape[0] - 1)]
    tile_owner = jnp.clip(tile_block // own_blocks, 0, parts - 1)
    tile_slot = member_of(jnp.where(is_own, me, tile_owner))

    onehot = tile_index[:, :, None] == jnp.arange(own_blocks, dtype=jnp.int32)[None, None, :]
    dense = jnp.sum(
        jnp.where(onehot[:, :, :, None, None], tile_weight[:, :, None].astype(F32), 0.0), axis=1
    )
    dense = dense.transpose(0, 2, 1, 3).reshape(owned, owned).astype(BF)
    row_total = jnp.sum(tile_weight, axis=(1, 3), dtype=F32).reshape(1, owned)
    inverse = 1.0 / row_total

    whole = lax.all_gather(side, "feat", axis=0, tiled=False)
    whole_feats = jnp.concatenate(
        [whole[:, i].reshape(-1, rows) for i in range(own_blocks)], axis=1
    )
    whole_cot = whole[:, own_blocks].reshape(-1, seeds)
    columns = lax.dynamic_index_in_dim(
        whole, own_blocks + 1 + lax.axis_index("feat"), 1, keepdims=False
    ).reshape(-1, 2 * width)

    named = jnp.any(halo_blocks == second, axis=1).astype(jnp.int32)
    named = jnp.where(jnp.arange(parts, dtype=jnp.int32) == me, 2, named)
    named = named[jnp.array(MEMBERS, dtype=jnp.int32)][:, None, None]
    history_t, named = lax.optimization_barrier((history.T, named))
    send_history = jnp.where(named == 1, history_t[None, :, rows:], history_t[None, :, :rows])
    send_history = jnp.where(named == 2, jnp.zeros((), BF), send_history)
    send_history, dense, inverse, tile_slot, halo_feats = lax.optimization_barrier(
        (send_history, dense, inverse, tile_slot, halo_feats)
    )
    halo_history = exchange(send_history)

    def halo_sum(picked):
        out = jnp.einsum("bkfc,bkvc->fbv", picked, tile_weight, preferred_element_type=F32)
        return out.reshape(width, owned)

    mean_one = (halo_sum(halo_feats[tile_slot]) + mm(feats_t, dense, ((1,), (1,)))) * inverse
    whole_mean_one = lax.all_gather(mean_one.astype(BF), "feat", axis=0, tiled=True)
    pre_one = mm(self_one_t, whole_feats, ((1,), (0,))) + mm(
        neigh_one_t, whole_mean_one, ((1,), (0,))
    )
    gate = jax.nn.sigmoid(pre_one)
    hidden = (pre_one * gate).astype(BF)

    seed_rows = (
        batch_ids[:, None] == jnp.arange(owned, dtype=jnp.int32)[None, :]
    ).astype(BF)
    whole_grad_two = mm(whole_cot, seed_rows, ((1,), (0,))).astype(BF)

    halo_history, hidden, whole_grad_two = lax.optimization_barrier(
        (halo_history, hidden, whole_grad_two)
    )
    mean_two = (
        (halo_sum(halo_history[tile_slot]) + mm(hidden, dense, ((1,), (1,)))) * inverse
    ).astype(BF)
    layer_two = jnp.concatenate([hidden, mean_two], axis=0)

    twos = mm(whole_grad_two, layer_two, ((1,), (1,))).astype(BF)
    twos, columns, pre_one, gate = lax.optimization_barrier((twos, columns, pre_one, gate))
    back = mm(columns, whole_grad_two, ((0,), (0,)))
    scaled = (back[width:] * inverse).astype(BF)
    own_grad = mm(scaled, dense, ((1,), (0,)))
    slope = gate * (1.0 + pre_one * (1.0 - gate))
    grad_one = ((back[:width] + own_grad) * slope).astype(BF)
    ones = mm(
        grad_one, jnp.concatenate([whole_feats, whole_mean_one], axis=0), ((1,), (1,))
    )
    depth = self_one.shape[0]
    lanes = 2 * width
    high = parts * lanes // (2 * depth)
    low = width // high
    ones = ones.astype(BF).reshape(high, low, 2 * depth // lanes, lanes).transpose(0, 2, 1, 3)
    ones = ones.reshape(parts, 1, low, lanes)
    twos = lax.all_to_all(twos.reshape(slices, width, 2 * width), "feat", 0, 0, tiled=True)
    layer_two, twos, ones = lax.optimization_barrier((layer_two, twos, ones))
    whole_two = lax.all_gather(layer_two, "feat", axis=0, tiled=False)
    pieces = jnp.concatenate([ones, twos.reshape(parts, 1, low, lanes)], axis=1)
    pieces = with_layout_constraint(pieces, Layout(major_to_minor=(0, 1, 2, 3)))
    got = exchange(pieces)
    mine = jnp.sum(got.astype(F32), axis=0, keepdims=True).astype(BF)
    spread = jnp.broadcast_to(mine, pieces.shape)
    sums = exchange(spread)
    grads = pl.pallas_call(
        unpack,
        in_specs=[pl.BlockSpec(memory_space=pl.ANY)],
        out_shape=[jax.ShapeDtypeStruct((width, depth), F32)] * 4,
        scratch_shapes=[pltpu.VMEM(sums.shape, BF)],
        compiler_params=pltpu.CompilerParams(vmem_limit_bytes=6 << 20),
    )(sums)

    whole_hidden = whole_two[:, :width].reshape(depth, owned)
    whole_mean_two = whole_two[:, width:].reshape(depth, owned)
    node_out = mm(self_two_t, whole_hidden, ((1,), (0,))) + mm(
        neigh_two_t, whole_mean_two, ((1,), (0,))
    )
    return (node_out.astype(BF).T, *[grad.T for grad in grads])


def solution(mesh):
    return jax.shard_map(
        on_device,
        mesh=mesh,
        in_specs=(
            P("dom", "feat"),
            P("dom", "feat"),
            P(),
            P("dom", None),
            P("dom", None, None, None),
            P(None, "feat"),
            P(None, "feat"),
            P(None, "feat"),
            P(None, "feat"),
            P("dom"),
            P("dom", "feat"),
        ),
        out_specs=(
            P("dom", "feat"),
            P(None, "feat"),
            P(None, "feat"),
            P(None, "feat"),
            P(None, "feat"),
        ),
        check_vma=False,
    )
```

```python
import jax
import jax.numpy as jnp
from jax import lax
from jax.experimental import pallas as pl
from jax.experimental.pallas import tpu as pltpu
from jax.experimental.layout import Layout, with_layout_constraint
from jax.sharding import PartitionSpec as P

BF = jnp.bfloat16
F32 = jnp.float32


def mm(a, b, dims):
    return lax.dot_general(a, b, (dims, ((), ())), preferred_element_type=F32)


CHUNKS = 4
SIDE = 8
MEMBERS = [(r % SIDE) * SIDE + (r // SIDE + r) % SIDE for r in range(SIDE * SIDE)]


BACKWARD = [MEMBERS[-r % len(MEMBERS)] for r in range(len(MEMBERS))]


def member_of(partition, turned):
    first, second = partition // SIDE, partition % SIDE
    place = (second - first + SIDE) % SIDE * SIDE + first
    return jnp.where(turned == 1, (len(MEMBERS) - place) % len(MEMBERS), place)


def exchange(pieces):
    feats = lax.axis_size("feat")
    groups = [
        [part * feats + feat for part in (BACKWARD if feat % 2 else MEMBERS)]
        for feat in range(feats)
    ]
    return lax.all_to_all(pieces, ("dom", "feat"), 0, 0, axis_index_groups=groups, tiled=True)


def lay_out(
    me_ref,
    halo_any,
    rows_any,
    seeds_any,
    self_any,
    neigh_any,
    out_any,
    side_any,
    halo_ref,
    rows_ref,
    seeds_ref,
    self_ref,
    neigh_ref,
    names_ref,
    picked,
    side_ref,
    in_sems,
    out_sems,
):
    def fetch(source, target, index):
        copy = pltpu.make_async_copy(source, target, in_sems.at[index])
        copy.start()
        return copy

    get_halo = fetch(halo_any, halo_ref, 0)
    get_rows = fetch(rows_any, rows_ref, 1)
    get_seeds = fetch(seeds_any, seeds_ref, 2)
    get_self = fetch(self_any, self_ref, 3)
    get_neigh = fetch(neigh_any, neigh_ref, 4)
    parts, width, lanes = picked.shape
    get_halo.wait()
    names = jnp.where(halo_ref[...] == 2 * me_ref[0] + 1, 1.0, 0.0)
    names = jnp.max(names, axis=0, keepdims=True)
    readers = lax.broadcasted_iota(jnp.int32, (1, parts), 1)
    names = jnp.where(readers == me_ref[0], 2.0, names)
    names_ref[...] = jnp.broadcast_to(names, (lanes, parts)).T
    get_rows.wait()
    low = rows_ref[:, :lanes].astype(F32)
    high = rows_ref[:, lanes:].astype(F32)
    step = parts // CHUNKS
    copies = []
    for chunk in range(CHUNKS):
        for reader in range(chunk * step, (chunk + 1) * step):
            named = jnp.where(me_ref[1] == 1, BACKWARD[reader], MEMBERS[reader])
            name = jnp.broadcast_to(names_ref[pl.ds(named, 1), :], low.shape)
            block = jnp.where(name > 1.5, 0.0, jnp.where(name > 0.5, high, low))
            picked[reader] = block.astype(picked.dtype)
        part = pl.ds(chunk * step, step)
        copy = pltpu.make_async_copy(picked.at[part], out_any.at[part], out_sems.at[chunk])
        copy.start()
        copies.append(copy)
    side_ref[0] = rows_ref[:, :lanes]
    side_ref[1] = rows_ref[:, lanes:]
    get_seeds.wait()
    side_ref[2] = seeds_ref[...]
    get_self.wait()
    get_neigh.wait()
    for pair in range(self_ref.shape[1] // lanes):
        across = slice(pair * lanes, (pair + 1) * lanes)
        own = self_ref[:, across].astype(F32)
        near = neigh_ref[:, across].astype(F32)
        left = jnp.concatenate([own[:, :width], near[:, :width]], axis=1)
        right = jnp.concatenate([own[:, width:], near[:, width:]], axis=1)
        side_ref[3 + 2 * pair] = left.astype(side_ref.dtype)
        side_ref[4 + 2 * pair] = right.astype(side_ref.dtype)
    copy = pltpu.make_async_copy(side_ref, side_any, out_sems.at[CHUNKS])
    copy.start()
    copies.append(copy)
    for copy in copies:
        copy.wait()


def unpack(sums_any, self_one_ref, neigh_one_ref, self_two_ref, neigh_two_ref, sums_ref):
    pltpu.sync_copy(sums_any, sums_ref)
    parts, _, low, lanes = sums_ref.shape
    width, depth = self_one_ref.shape
    high = width // low
    wide = depth // lanes
    for i in range(high):
        down = slice(i * low, (i + 1) * low)
        for j in range(wide):
            across = slice(j * lanes, (j + 1) * lanes)
            base = i * 2 * wide + j
            self_one_ref[down, across] = sums_ref[base, 0].astype(F32)
            neigh_one_ref[down, across] = sums_ref[base + wide, 0].astype(F32)
            left = sums_ref[2 * j * high + i, 1].astype(F32)
            right = sums_ref[(2 * j + 1) * high + i, 1].astype(F32)
            self_two_ref[down, across] = jnp.concatenate(
                [left[:, :width], right[:, :width]], axis=1
            )
            neigh_two_ref[down, across] = jnp.concatenate(
                [left[:, width:], right[:, width:]], axis=1
            )


def on_device(
    node_feats,
    history,
    halo_blocks,
    tile_index,
    tile_weight,
    self_one,
    neigh_one,
    self_two,
    neigh_two,
    batch_ids,
    cotangent,
):
    own_blocks, tiles = tile_index.shape
    rows = tile_weight.shape[2]
    width = node_feats.shape[1]
    owned = node_feats.shape[0]
    parts = halo_blocks.shape[0]
    seeds = cotangent.shape[0]
    me = lax.axis_index("dom")
    turned = lax.axis_index("feat") % 2

    feats_t = node_feats.T
    cot_t = cotangent.T
    self_one_t, neigh_one_t, self_two_t, neigh_two_t = (
        self_one.T,
        neigh_one.T,
        self_two.T,
        neigh_two.T,
    )

    second = own_blocks * me + 1
    slices = self_two_t.shape[1] // width
    side_shape = (own_blocks + 1 + slices, width, rows)
    operands = (halo_blocks.T, feats_t, cot_t, self_two_t, neigh_two_t)
    send_feats, side = pl.pallas_call(
        lay_out,
        in_specs=[pl.BlockSpec(memory_space=pltpu.SMEM)]
        + [pl.BlockSpec(memory_space=pl.ANY)] * len(operands),
        out_specs=[pl.BlockSpec(memory_space=pl.ANY)] * 2,
        out_shape=[
            jax.ShapeDtypeStruct((parts, width, rows), BF),
            jax.ShapeDtypeStruct(side_shape, BF),
        ],
        scratch_shapes=[pltpu.VMEM(operand.shape, operand.dtype) for operand in operands]
        + [
            pltpu.VMEM((parts, rows), F32),
            pltpu.VMEM((parts, width, rows), BF),
            pltpu.VMEM(side_shape, BF),
            pltpu.SemaphoreType.DMA((len(operands),)),
            pltpu.SemaphoreType.DMA((CHUNKS + 1,)),
        ],
    )(jnp.stack([me, turned]).astype(jnp.int32), *operands)
    halo_feats = exchange(send_feats)
    wanted = lax.dynamic_index_in_dim(halo_blocks, me, 0, keepdims=False)
    is_own = tile_index < own_blocks
    tile_block = wanted[jnp.clip(tile_index - own_blocks, 0, wanted.shape[0] - 1)]
    tile_owner = jnp.clip(tile_block // own_blocks, 0, parts - 1)
    tile_slot = member_of(jnp.where(is_own, me, tile_owner), turned)

    onehot = tile_index[:, :, None] == jnp.arange(own_blocks, dtype=jnp.int32)[None, None, :]
    dense = jnp.sum(
        jnp.where(onehot[:, :, :, None, None], tile_weight[:, :, None].astype(F32), 0.0), axis=1
    )
    dense = dense.transpose(0, 2, 1, 3).reshape(owned, owned).astype(BF)
    row_total = jnp.sum(tile_weight, axis=(1, 3), dtype=F32).reshape(1, owned)
    inverse = 1.0 / row_total

    whole = lax.all_gather(side, "feat", axis=0, tiled=False)
    whole_feats = jnp.concatenate(
        [whole[:, i].reshape(-1, rows) for i in range(own_blocks)], axis=1
    )
    whole_cot = whole[:, own_blocks].reshape(-1, seeds)
    columns = lax.dynamic_index_in_dim(
        whole, own_blocks + 1 + lax.axis_index("feat"), 1, keepdims=False
    ).reshape(-1, 2 * width)

    named = jnp.any(halo_blocks == second, axis=1).astype(jnp.int32)
    named = jnp.where(jnp.arange(parts, dtype=jnp.int32) == me, 2, named)
    order = jnp.where(
        turned == 1, jnp.array(BACKWARD, dtype=jnp.int32), jnp.array(MEMBERS, dtype=jnp.int32)
    )
    named = named[order][:, None, None]
    history_t, named = lax.optimization_barrier((history.T, named))
    send_history = jnp.where(named == 1, history_t[None, :, rows:], history_t[None, :, :rows])
    send_history = jnp.where(named == 2, jnp.zeros((), BF), send_history)
    send_history, dense, inverse, tile_slot, halo_feats = lax.optimization_barrier(
        (send_history, dense, inverse, tile_slot, halo_feats)
    )
    halo_history = exchange(send_history)

    def halo_sum(picked):
        out = jnp.einsum("bkfc,bkvc->fbv", picked, tile_weight, preferred_element_type=F32)
        return out.reshape(width, owned)

    mean_one = (halo_sum(halo_feats[tile_slot]) + mm(feats_t, dense, ((1,), (1,)))) * inverse
    whole_mean_one = lax.all_gather(mean_one.astype(BF), "feat", axis=0, tiled=True)
    pre_one = mm(self_one_t, whole_feats, ((1,), (0,))) + mm(
        neigh_one_t, whole_mean_one, ((1,), (0,))
    )
    gate = jax.nn.sigmoid(pre_one)
    hidden = (pre_one * gate).astype(BF)

    seed_rows = (
        batch_ids[:, None] == jnp.arange(owned, dtype=jnp.int32)[None, :]
    ).astype(BF)
    whole_grad_two = mm(whole_cot, seed_rows, ((1,), (0,))).astype(BF)

    halo_history, hidden, whole_grad_two = lax.optimization_barrier(
        (halo_history, hidden, whole_grad_two)
    )
    mean_two = (
        (halo_sum(halo_history[tile_slot]) + mm(hidden, dense, ((1,), (1,)))) * inverse
    ).astype(BF)
    layer_two = jnp.concatenate([hidden, mean_two], axis=0)

    twos = mm(whole_grad_two, layer_two, ((1,), (1,))).astype(BF)
    twos, columns, pre_one, gate = lax.optimization_barrier((twos, columns, pre_one, gate))
    back = mm(columns, whole_grad_two, ((0,), (0,)))
    scaled = (back[width:] * inverse).astype(BF)
    own_grad = mm(scaled, dense, ((1,), (0,)))
    slope = gate * (1.0 + pre_one * (1.0 - gate))
    grad_one = ((back[:width] + own_grad) * slope).astype(BF)
    ones = mm(
        grad_one, jnp.concatenate([whole_feats, whole_mean_one], axis=0), ((1,), (1,))
    )
    depth = self_one.shape[0]
    lanes = 2 * width
    high = parts * lanes // (2 * depth)
    low = width // high
    ones = ones.astype(BF).reshape(high, low, 2 * depth // lanes, lanes).transpose(0, 2, 1, 3)
    ones = ones.reshape(parts, 1, low, lanes)
    twos = lax.all_to_all(twos.reshape(slices, width, 2 * width), "feat", 0, 0, tiled=True)
    layer_two, twos, ones = lax.optimization_barrier((layer_two, twos, ones))
    whole_two = lax.all_gather(layer_two, "feat", axis=0, tiled=False)
    pieces = jnp.concatenate([ones, twos.reshape(parts, 1, low, lanes)], axis=1)
    pieces = with_layout_constraint(pieces, Layout(major_to_minor=(0, 1, 2, 3)))
    got = exchange(pieces)
    mine = jnp.sum(got.astype(F32), axis=0, keepdims=True).astype(BF)
    spread = jnp.broadcast_to(mine, pieces.shape)
    sums = exchange(spread)
    grads = pl.pallas_call(
        unpack,
        in_specs=[pl.BlockSpec(memory_space=pl.ANY)],
        out_shape=[jax.ShapeDtypeStruct((width, depth), F32)] * 4,
        scratch_shapes=[pltpu.VMEM(sums.shape, BF)],
        compiler_params=pltpu.CompilerParams(vmem_limit_bytes=6 << 20),
    )(sums)

    whole_hidden = whole_two[:, :width].reshape(depth, owned)
    whole_mean_two = whole_two[:, width:].reshape(depth, owned)
    node_out = mm(self_two_t, whole_hidden, ((1,), (0,))) + mm(
        neigh_two_t, whole_mean_two, ((1,), (0,))
    )
    return (node_out.astype(BF).T, *[grad.T for grad in grads])


def solution(mesh):
    return jax.shard_map(
        on_device,
        mesh=mesh,
        in_specs=(
            P("dom", "feat"),
            P("dom", "feat"),
            P(),
            P("dom", None),
            P("dom", None, None, None),
            P(None, "feat"),
            P(None, "feat"),
            P(None, "feat"),
            P(None, "feat"),
            P("dom"),
            P("dom", "feat"),
        ),
        out_specs=(
            P("dom", "feat"),
            P(None, "feat"),
            P(None, "feat"),
            P(None, "feat"),
            P(None, "feat"),
        ),
        check_vma=False,
    )
```

```python
import jax
import jax.numpy as jnp
from jax import lax
from jax.experimental import pallas as pl
from jax.experimental.pallas import tpu as pltpu
from jax.experimental.layout import Layout, with_layout_constraint
from jax.sharding import PartitionSpec as P

BF = jnp.bfloat16
F32 = jnp.float32


def mm(a, b, dims):
    return lax.dot_general(a, b, (dims, ((), ())), preferred_element_type=F32)


CHUNKS = 4
SIDE = 8
MEMBERS = [(r % SIDE) * SIDE + (r // SIDE + r) % SIDE for r in range(SIDE * SIDE)]


def member_of(partition):
    first, second = partition // SIDE, partition % SIDE
    return (second - first + SIDE) % SIDE * SIDE + first


def exchange(pieces):
    return lax.all_to_all(pieces, "dom", 0, 0, axis_index_groups=[MEMBERS], tiled=True)


def lay_out(
    me_ref,
    halo_any,
    rows_any,
    seeds_any,
    self_any,
    neigh_any,
    out_any,
    side_any,
    halo_ref,
    rows_ref,
    seeds_ref,
    self_ref,
    neigh_ref,
    picked,
    side_ref,
    in_sems,
    out_sems,
):
    def fetch(source, target, index):
        copy = pltpu.make_async_copy(source, target, in_sems.at[index])
        copy.start()
        return copy

    get_halo = fetch(halo_any, halo_ref, 0)
    get_rows = fetch(rows_any, rows_ref, 1)
    get_seeds = fetch(seeds_any, seeds_ref, 2)
    get_self = fetch(self_any, self_ref, 3)
    get_neigh = fetch(neigh_any, neigh_ref, 4)
    parts, width, lanes = picked.shape
    get_halo.wait()
    names = jnp.where(halo_ref[...] == 2 * me_ref[0] + 1, 1.0, 0.0)
    names = jnp.max(names, axis=0, keepdims=True)
    readers = lax.broadcasted_iota(jnp.int32, (1, parts), 1)
    names = jnp.where(readers == me_ref[0], 2.0, names)
    names = jnp.broadcast_to(names, (lanes, parts)).T
    get_rows.wait()
    low = rows_ref[:, :lanes].astype(F32)
    high = rows_ref[:, lanes:].astype(F32)
    step = parts // CHUNKS
    copies = []
    for chunk in range(CHUNKS):
        for reader in range(chunk * step, (chunk + 1) * step):
            named = MEMBERS[reader]
            name = jnp.broadcast_to(names[named : named + 1, :], low.shape)
            block = jnp.where(name > 1.5, 0.0, jnp.where(name > 0.5, high, low))
            picked[reader] = block.astype(picked.dtype)
        part = pl.ds(chunk * step, step)
        copy = pltpu.make_async_copy(picked.at[part], out_any.at[part], out_sems.at[chunk])
        copy.start()
        copies.append(copy)
    side_ref[0] = rows_ref[:, :lanes]
    side_ref[1] = rows_ref[:, lanes:]
    get_seeds.wait()
    side_ref[2] = seeds_ref[...]
    get_self.wait()
    get_neigh.wait()
    for pair in range(self_ref.shape[1] // lanes):
        across = slice(pair * lanes, (pair + 1) * lanes)
        own = self_ref[:, across].astype(F32)
        near = neigh_ref[:, across].astype(F32)
        left = jnp.concatenate([own[:, :width], near[:, :width]], axis=1)
        right = jnp.concatenate([own[:, width:], near[:, width:]], axis=1)
        side_ref[3 + 2 * pair] = left.astype(side_ref.dtype)
        side_ref[4 + 2 * pair] = right.astype(side_ref.dtype)
    copy = pltpu.make_async_copy(side_ref, side_any, out_sems.at[CHUNKS])
    copy.start()
    copies.append(copy)
    for copy in copies:
        copy.wait()


def unpack(sums_any, self_one_ref, neigh_one_ref, self_two_ref, neigh_two_ref, sums_ref):
    pltpu.sync_copy(sums_any, sums_ref)
    parts, _, low, lanes = sums_ref.shape
    width, depth = self_one_ref.shape
    high = width // low
    wide = depth // lanes
    for i in range(high):
        down = slice(i * low, (i + 1) * low)
        for j in range(wide):
            across = slice(j * lanes, (j + 1) * lanes)
            base = i * 2 * wide + j
            self_one_ref[down, across] = sums_ref[base, 0].astype(F32)
            neigh_one_ref[down, across] = sums_ref[base + wide, 0].astype(F32)
            left = sums_ref[2 * j * high + i, 1].astype(F32)
            right = sums_ref[(2 * j + 1) * high + i, 1].astype(F32)
            self_two_ref[down, across] = jnp.concatenate(
                [left[:, :width], right[:, :width]], axis=1
            )
            neigh_two_ref[down, across] = jnp.concatenate(
                [left[:, width:], right[:, width:]], axis=1
            )


def on_device(
    node_feats,
    history,
    halo_blocks,
    tile_index,
    tile_weight,
    self_one,
    neigh_one,
    self_two,
    neigh_two,
    batch_ids,
    cotangent,
):
    own_blocks, tiles = tile_index.shape
    rows = tile_weight.shape[2]
    width = node_feats.shape[1]
    owned = node_feats.shape[0]
    parts = halo_blocks.shape[0]
    seeds = cotangent.shape[0]
    me = lax.axis_index("dom")

    feats_t = node_feats.T
    cot_t = cotangent.T
    self_one_t, neigh_one_t, self_two_t, neigh_two_t = (
        self_one.T,
        neigh_one.T,
        self_two.T,
        neigh_two.T,
    )

    second = own_blocks * me + 1
    slices = self_two_t.shape[1] // width
    side_shape = (own_blocks + 1 + slices, width, rows)
    operands = (halo_blocks.T, feats_t, cot_t, self_two_t, neigh_two_t)
    send_feats, side = pl.pallas_call(
        lay_out,
        in_specs=[pl.BlockSpec(memory_space=pltpu.SMEM)]
        + [pl.BlockSpec(memory_space=pl.ANY)] * len(operands),
        out_specs=[pl.BlockSpec(memory_space=pl.ANY)] * 2,
        out_shape=[
            jax.ShapeDtypeStruct((parts, width, rows), BF),
            jax.ShapeDtypeStruct(side_shape, BF),
        ],
        scratch_shapes=[pltpu.VMEM(operand.shape, operand.dtype) for operand in operands]
        + [
            pltpu.VMEM((parts, width, rows), BF),
            pltpu.VMEM(side_shape, BF),
            pltpu.SemaphoreType.DMA((len(operands),)),
            pltpu.SemaphoreType.DMA((CHUNKS + 1,)),
        ],
    )(me.reshape(1).astype(jnp.int32), *operands)
    halo_feats = exchange(send_feats)
    wanted = lax.dynamic_index_in_dim(halo_blocks, me, 0, keepdims=False)
    is_own = tile_index < own_blocks
    tile_block = wanted[jnp.clip(tile_index - own_blocks, 0, wanted.shape[0] - 1)]
    tile_owner = jnp.clip(tile_block // own_blocks, 0, parts - 1)
    tile_slot = member_of(jnp.where(is_own, me, tile_owner))

    onehot = tile_index[:, :, None] == jnp.arange(own_blocks, dtype=jnp.int32)[None, None, :]
    dense = jnp.sum(
        jnp.where(onehot[:, :, :, None, None], tile_weight[:, :, None].astype(F32), 0.0), axis=1
    )
    dense = dense.transpose(0, 2, 1, 3).reshape(owned, owned).astype(BF)
    row_total = jnp.sum(tile_weight, axis=(1, 3), dtype=F32).reshape(1, owned)
    inverse = 1.0 / row_total

    whole = lax.all_gather(side, "feat", axis=0, tiled=False)
    whole_feats = jnp.concatenate(
        [whole[:, i].reshape(-1, rows) for i in range(own_blocks)], axis=1
    )
    whole_cot = whole[:, own_blocks].reshape(-1, seeds)
    columns = lax.dynamic_index_in_dim(
        whole, own_blocks + 1 + lax.axis_index("feat"), 1, keepdims=False
    ).reshape(-1, 2 * width)

    named = jnp.any(halo_blocks == second, axis=1).astype(jnp.int32)
    named = jnp.where(jnp.arange(parts, dtype=jnp.int32) == me, 2, named)
    named = named[jnp.array(MEMBERS, dtype=jnp.int32)][:, None, None]
    history_t, named = lax.optimization_barrier((history.T, named))
    send_history = jnp.where(named == 1, history_t[None, :, rows:], history_t[None, :, :rows])
    send_history = jnp.where(named == 2, jnp.zeros((), BF), send_history)
    send_history, dense, inverse, tile_slot, halo_feats = lax.optimization_barrier(
        (send_history, dense, inverse, tile_slot, halo_feats)
    )
    halo_history = exchange(send_history)

    def halo_sum(picked):
        out = jnp.einsum("bkfc,bkvc->fbv", picked, tile_weight, preferred_element_type=F32)
        return out.reshape(width, owned)

    mean_one = (halo_sum(halo_feats.at[tile_slot].get(mode="promise_in_bounds")) + mm(feats_t, dense, ((1,), (1,)))) * inverse
    whole_mean_one = lax.all_gather(mean_one.astype(BF), "feat", axis=0, tiled=True)
    pre_one = mm(self_one_t, whole_feats, ((1,), (0,))) + mm(
        neigh_one_t, whole_mean_one, ((1,), (0,))
    )
    gate = jax.nn.sigmoid(pre_one)
    hidden = (pre_one * gate).astype(BF)

    seed_rows = (
        batch_ids[:, None] == jnp.arange(owned, dtype=jnp.int32)[None, :]
    ).astype(BF)
    whole_grad_two = mm(whole_cot, seed_rows, ((1,), (0,))).astype(BF)

    halo_history, hidden, whole_grad_two = lax.optimization_barrier(
        (halo_history, hidden, whole_grad_two)
    )
    mean_two = (
        (halo_sum(halo_history.at[tile_slot].get(mode="promise_in_bounds")) + mm(hidden, dense, ((1,), (1,)))) * inverse
    ).astype(BF)
    layer_two = jnp.concatenate([hidden, mean_two], axis=0)

    twos = mm(whole_grad_two, layer_two, ((1,), (1,))).astype(BF)
    twos, columns, pre_one, gate = lax.optimization_barrier((twos, columns, pre_one, gate))
    back = mm(columns, whole_grad_two, ((0,), (0,)))
    scaled = (back[width:] * inverse).astype(BF)
    own_grad = mm(scaled, dense, ((1,), (0,)))
    slope = gate * (1.0 + pre_one * (1.0 - gate))
    grad_one = ((back[:width] + own_grad) * slope).astype(BF)
    ones = mm(
        grad_one, jnp.concatenate([whole_feats, whole_mean_one], axis=0), ((1,), (1,))
    )
    depth = self_one.shape[0]
    lanes = 2 * width
    high = parts * lanes // (2 * depth)
    low = width // high
    ones = ones.astype(BF).reshape(high, low, 2 * depth // lanes, lanes).transpose(0, 2, 1, 3)
    ones = ones.reshape(parts, 1, low, lanes)
    twos = lax.all_to_all(twos.reshape(slices, width, 2 * width), "feat", 0, 0, tiled=True)
    layer_two, twos, ones = lax.optimization_barrier((layer_two, twos, ones))
    whole_two = lax.all_gather(layer_two, "feat", axis=0, tiled=False)
    pieces = jnp.concatenate([ones, twos.reshape(parts, 1, low, lanes)], axis=1)
    pieces = with_layout_constraint(pieces, Layout(major_to_minor=(0, 1, 2, 3)))
    got = exchange(pieces)
    mine = jnp.sum(got.astype(F32), axis=0, keepdims=True).astype(BF)
    spread = jnp.broadcast_to(mine, pieces.shape)
    sums = exchange(spread)
    grads = pl.pallas_call(
        unpack,
        in_specs=[pl.BlockSpec(memory_space=pl.ANY)],
        out_shape=[jax.ShapeDtypeStruct((width, depth), F32)] * 4,
        scratch_shapes=[pltpu.VMEM(sums.shape, BF)],
        compiler_params=pltpu.CompilerParams(vmem_limit_bytes=6 << 20),
    )(sums)

    whole_hidden = whole_two[:, :width].reshape(depth, owned)
    whole_mean_two = whole_two[:, width:].reshape(depth, owned)
    node_out = mm(self_two_t, whole_hidden, ((1,), (0,))) + mm(
        neigh_two_t, whole_mean_two, ((1,), (0,))
    )
    return (node_out.astype(BF).T, *[grad.T for grad in grads])


def solution(mesh):
    return jax.shard_map(
        on_device,
        mesh=mesh,
        in_specs=(
            P("dom", "feat"),
            P("dom", "feat"),
            P(),
            P("dom", None),
            P("dom", None, None, None),
            P(None, "feat"),
            P(None, "feat"),
            P(None, "feat"),
            P(None, "feat"),
            P("dom"),
            P("dom", "feat"),
        ),
        out_specs=(
            P("dom", "feat"),
            P(None, "feat"),
            P(None, "feat"),
            P(None, "feat"),
            P(None, "feat"),
        ),
        check_vma=False,
    )
```
